128 devices in a mesh: section: 2 (over core), dp: 8 (over x_hi, z), mp: 8 (over x_lo, y).
Axes of the slice: x: 4 (x_hi: 2, x_lo: 2; x = x_hi * 2 + x_lo), y: 4, z: 4, core: 2. Of those that a mesh axis runs over, the one named last changes fastest.
Arguments:
- fwd_in: bfloat16 [2, 8, 8, 256, 1536], P('section', 'dp', 'mp'), may hold values from -6 to 6
- kept_in: bfloat16 [2, 8, 8, 256, 1536], P('section', 'dp', 'mp'), may hold values from -6 to 6
- cotangent: bfloat16 [2, 8, 8, 256, 1536], P('section', 'dp', 'mp'), may hold values from -6 to 6
- weight: bfloat16 [2, 12288, 12288], P('section', 'mp', 'dp'), may hold values from -1 to 1
- bias: float32 [2, 12288], P('section', 'dp'), may hold values from -3 to 3
- norm_gain: float32 [2, 12288], P('section', 'mp'), may hold values from 0.1 to 1.9
- norm_shift: float32 [2, 12288], P('section', 'mp'), may hold values from -3 to 3
Outputs:
- next_in: bfloat16 [2, 8, 8, 256, 1536], P('section', 'dp', 'mp')
- passed: bfloat16 [2, 8, 8, 256, 1536], P('section', 'dp', 'mp')
- weight_grad: float32 [2, 12288, 12288], P('section', 'mp', 'dp')
- bias_grad: float32 [2, 12288], P('section', 'dp')
- norm_grads: float32 [2, 2, 12288], P('section', None, 'mp')
The draws below stay inside these ranges and needn't reach their ends.
All inputs are finite; a program needn't handle non-finite values.
Results may differ from the reference program's by a relative error of at most 0.018.
Values may be sent and summed in bfloat16 or wider, within the bound.
A program may use at most 128 MiB of HBM per device.

```python
import jax
import jax.numpy as jnp
from jax import lax

D = 12288
POS = 256
TOKENS = 2048
N_DP = 8
N_MP = 8


def tilted_matrix(key, noise, low_end, high_end):
    sign_key, rough_key = jax.random.split(key)
    signs = jnp.where(jax.random.bernoulli(sign_key, 0.5, (2, 1, D)), 1.0, -1.0).astype(jnp.float32)
    place = jnp.arange(D, dtype=jnp.float32) / (D - 1)
    rising = jnp.exp(jnp.log(low_end) + (jnp.log(high_end) - jnp.log(low_end)) * place)
    rough = jax.random.uniform(rough_key, (2, D, D), jnp.float32, 0.6, 1.4)
    common = 0.15 * signs * rising[None, :, None] * rough
    return ((noise + common) * D ** (-0.5)).astype(jnp.bfloat16)


def draw_weight(key, part):
    key = jax.random.fold_in(key, 11)
    noise_key, tilt_key = jax.random.split(key)
    noise = jnp.clip(jax.random.normal(noise_key, (2, D, D), jnp.float32), -6.0, 6.0)
    return tilted_matrix(tilt_key, noise, 0.3, 3.0)


def steps_of(key, shape, cuts, smallest, top_value):
    loudness, own = 1.0, jax.random.fold_in(key, 6)
    for axis_at, parts in cuts:
        steps = jnp.exp(jax.random.uniform(jax.random.fold_in(own, axis_at), (parts,), jnp.float32, smallest / len(cuts), top_value / len(cuts)))
        loudness = loudness * jnp.repeat(steps, shape[axis_at] // parts).reshape([-1 if axis == axis_at else 1 for axis in range(len(shape))])
    return loudness


def centred(rng, dims, scale, most, shards=(), kind=jnp.bfloat16):
    gain = steps_of(rng, dims, shards, -0.22, 0.18) if shards else 1.0
    result = jax.random.normal(rng, dims, jnp.float32) * scale * gain
    return jnp.minimum(jnp.maximum(result, -most), most).astype(kind)


def setup_inputs(seed: int = 0) -> dict:
    key_list = jax.random.split(jax.random.key(seed), 8)
    fwd_in = centred(key_list[0], (2, N_DP, N_MP, POS, D // N_MP), 1.0, 6.0, ((0, 2), (1, 8), (2, 8)))
    kept_in = centred(key_list[1], (2, N_DP, N_MP, POS, D // N_MP), 1.0, 6.0, ((0, 2), (1, 8), (2, 8)))
    cotangent = centred(key_list[2], (2, N_DP, N_MP, POS, D // N_MP), 1.0, 6.0, ((0, 2), (1, 8), (2, 8)))
    weight = draw_weight(jax.random.fold_in(key_list[7], 71), 0)
    bias = centred(key_list[4], (2, D), 0.5, 3.0, ((0, 2), (1, 8)), jnp.float32)
    norm_gain = jnp.clip(1.0 + 0.18 * jax.random.normal(key_list[5], (2, D), jnp.float32), 0.1, 1.9)
    norm_shift = centred(key_list[6], (2, D), 0.5, 3.0, ((0, 2), (1, 8)), jnp.float32)
    return dict(fwd_in=fwd_in, kept_in=kept_in, cotangent=cotangent, weight=weight, bias=bias, norm_gain=norm_gain, norm_shift=norm_shift)


eps = 1e-05

def from_in(blocks):
    return blocks.transpose(0, 2, 1, 3).reshape(TOKENS, D)

def from_out(blocks):
    return blocks.transpose(1, 2, 0, 3).reshape(TOKENS, D)

def to_in(matrix):
    return matrix.reshape(N_DP, POS, N_MP, D // N_MP).transpose(0, 2, 1, 3)

def to_out(matrix):
    return matrix.reshape(N_MP, POS, N_DP, D // N_MP).transpose(2, 0, 1, 3)

def relabel(matrix):
    shaped = matrix.reshape(N_DP, N_DP, POS // N_DP, N_MP, N_MP, D // (N_MP * N_MP))
    return shaped.transpose(1, 0, 2, 4, 3, 5).reshape(TOKENS, D)

def normalize(values, gain_row, shift_row):
    floats = values.astype(jnp.float32)
    mean_val = lax.optimization_barrier(jnp.mean(floats, 1, keepdims=True))
    spread = lax.optimization_barrier(jnp.mean(floats * floats, 1, keepdims=True)) - mean_val * mean_val
    inverse = lax.rsqrt(spread + eps)
    normal = (floats - mean_val) * inverse
    return (normal, inverse, (normal * gain_row + shift_row).astype(jnp.bfloat16))

def rounded(values):
    return lax.optimization_barrier(values.astype(jnp.bfloat16)).astype(jnp.float32)

def section_pass(fresh_rows, kept_rows, upstream, weight_full, bias_row, gain_row, shift_row):
    block_width = D // N_MP
    normal_x, inverse_x, normed = normalize(fresh_rows, gain_row, shift_row)
    normal_k, inverse_k, normed_kept = normalize(kept_rows, gain_row, shift_row)
    summed = jnp.zeros((TOKENS, D), jnp.float32)
    for block in range(N_MP):
        low = block * block_width
        term = jnp.dot(normed[:, low:low + block_width], weight_full[low:low + block_width], preferred_element_type=jnp.float32)
        summed = summed + rounded(term)
    output = (summed + bias_row[None, :]).astype(jnp.bfloat16)
    weight_grad = lax.dot_general(normed_kept, upstream, (((0,), (0,)), ((), ())), preferred_element_type=jnp.float32)
    bias_grad = lax.optimization_barrier(jnp.sum(upstream.astype(jnp.float32), 0))
    grad_rows = jnp.zeros((TOKENS, D), jnp.float32)
    for block in range(N_DP):
        low = block * block_width
        term = lax.dot_general(upstream[:, low:low + block_width], weight_full[:, low:low + block_width], (((1,), (1,)), ((), ())), preferred_element_type=jnp.float32)
        grad_rows = grad_rows + rounded(term)
    gain_grad = lax.optimization_barrier(jnp.sum(grad_rows * normal_k, 0))
    shift_grad = lax.optimization_barrier(jnp.sum(grad_rows, 0))
    scaled = grad_rows * gain_row[None, :]
    first_mean = lax.optimization_barrier(jnp.mean(scaled, 1, keepdims=True))
    second_mean = lax.optimization_barrier(jnp.mean(scaled * normal_k, 1, keepdims=True))
    input_grad = (inverse_k * (scaled - first_mean - normal_k * second_mean)).astype(jnp.bfloat16)
    return (output, input_grad, weight_grad, bias_grad, jnp.stack([gain_grad, shift_grad]))

def reference(fwd_in, kept_in, cotangent, weight, bias, norm_gain, norm_shift):
    results = []
    for section_slot in range(2):
        results.append(section_pass(from_in(fwd_in[section_slot]), from_in(kept_in[section_slot]), from_out(cotangent[section_slot]), weight[section_slot], bias[section_slot].astype(jnp.float32), norm_gain[section_slot].astype(jnp.float32), norm_shift[section_slot].astype(jnp.float32)))
    first, second = (results[0], results[1])
    next_in = jnp.stack([to_out(relabel(second[1])), to_in(relabel(first[0]))])
    passed = jnp.stack([to_in(first[1]), to_out(second[0])])
    weight_grad = jnp.stack([first[2], second[2]])
    bias_grad = jnp.stack([first[3], second[3]])
    norm_grads = jnp.stack([first[4], second[4]])
    return (next_in, passed, weight_grad, bias_grad, norm_grads)
```

```python
import jax
import jax.numpy as jnp
from jax import lax
from jax.experimental import pallas as pl
from jax.experimental.pallas import tpu as pltpu
from jax.sharding import PartitionSpec as P

EPS = 1e-05
RING = 4
PAIR = 2
GROUP = RING * PAIR
TILE = 16
MXU = 256
F32 = jnp.float32
BF16 = jnp.bfloat16
MESH = pl.DeviceIdType.MESH


class Spot:
    def __init__(self, group):
        self.group = group
        self.index = lax.axis_index(group)
        self.pair = lax.div(self.index, RING)
        self.ring = lax.rem(self.index, RING)

    def slot(self, pair_step, ring_step):
        pair = lax.rem(self.pair + pair_step, PAIR)
        return pair * RING + lax.rem(self.ring + ring_step + RING, RING)

    def device(self, pair_step, ring_step):
        return {self.group: self.slot(pair_step, ring_step)}


class Gather:
    def __init__(self, spot, buf, send_sem, recv_sem, far_by_pair):
        self.spot, self.buf, self.far_by_pair = spot, buf, far_by_pair
        self.send_sem, self.recv_sem = send_sem, recv_sem
        self.half = buf.shape[1] // 2
        self.started = []

    def route(self, kind, c):
        step = 1 if c == 0 else -1
        return {
            0: ((0, 0), (1, 0), (1, 0)),
            1: ((0, 0), (0, 1), (0, -1)),
            2: ((0, 0), (0, -1), (0, 1)),
            3: ((1, 0), (0, 1), (1, -1)),
            4: ((1, 0), (0, -1), (1, 1)),
            5: ((0, -step), (0, step), (0, 2)),
            6: ((0, 2), (1, 0), (1, 2)) if self.far_by_pair else ((1, -step), (0, step), (1, 2)),
        }[kind]

    def copy(self, kind, c, landing):
        source, target, lands = self.route(kind, c)
        here = self.spot.slot(*(lands if landing else source))
        view = self.buf.at[here, pl.ds(c * self.half, self.half)]
        return pltpu.make_async_remote_copy(
            src_ref=view,
            dst_ref=view,
            send_sem=self.send_sem.at[kind, c],
            recv_sem=self.recv_sem.at[kind, c],
            device_id=self.spot.device(*target),
            device_id_type=MESH,
        )

    def start(self, kind, c):
        self.copy(kind, c, False).start()
        self.started.append((kind, c))

    def arrived(self, kind, c):
        self.copy(kind, c, True).wait_recv()

    def finish(self):
        for kind, c in self.started:
            self.copy(kind, c, False).wait_send()
        self.started = []


class Scatter:
    def __init__(self, spot, stage, halves, left, right, crossed, send_sem, recv_sem):
        self.spot, self.stage = spot, stage
        self.halves, self.left, self.right, self.crossed = halves, left, right, crossed
        self.send_sem, self.recv_sem = send_sem, recv_sem
        self.half = halves.shape[1] // 2
        self.started = []

    def copy(self, kind, side, c):
        spot, rows = self.spot, pl.ds(c * self.half, self.half)
        step = 1 if c == 0 else -1
        source, target, lands = {
            0: (self.stage(side, 2), (0, step), self.halves.at[side]),
            1: (self.stage(side, 1), (0, 1), self.left.at[side]),
            2: (self.stage(side, -1), (0, -1), self.right.at[side]),
            3: (self.stage(side, 0), (1, 0), self.crossed),
        }[kind]
        sem = (kind * 2 + side) * 2 + c
        return pltpu.make_async_remote_copy(
            src_ref=source.at[rows],
            dst_ref=lands.at[rows],
            send_sem=self.send_sem.at[sem],
            recv_sem=self.recv_sem.at[sem],
            device_id=spot.device(*target),
            device_id_type=MESH,
        )

    def start(self, kind, side, c):
        self.copy(kind, side, c).start()
        self.started.append((kind, side, c))

    def arrived(self, kind, side, c):
        self.copy(kind, side, c).wait_recv()

    def finish(self):
        for key in self.started:
            self.copy(*key).wait_send()
        self.started = []


class Spread:
    def __init__(self, spot, buf, send_sem, recv_sem):
        self.spot, self.buf, self.send_sem, self.recv_sem = spot, buf, send_sem, recv_sem

    def copy(self, step, landing):
        me = self.spot.index
        other = lax.rem(me + step, GROUP)
        view = self.buf.at[lax.rem(me + GROUP - step, GROUP) if landing else me]
        return pltpu.make_async_remote_copy(
            src_ref=view,
            dst_ref=view,
            send_sem=self.send_sem.at[step - 1],
            recv_sem=self.recv_sem.at[step - 1],
            device_id={self.spot.group: other},
            device_id_type=MESH,
        )

    def start(self):
        for step in range(1, GROUP):
            self.copy(step, False).start()

    def arrived(self):
        for step in range(1, GROUP):
            self.copy(step, True).wait_recv()

    def finish(self):
        for step in range(1, GROUP):
            self.copy(step, False).wait_send()

    def total(self):
        result = self.buf[0]
        for i in range(1, GROUP):
            result = result + self.buf[i]
        return result


def tiles(count, body, size=TILE):
    def step(i, carry):
        body(pl.ds(pl.multiple_of(i * size, size), size))
        return carry

    lax.fori_loop(0, count // size, step, 0)


def relay_kernel(
    fwd, kept, cot, weight, bias, gain, shift,
    arrived_out, passed_out, wg_out, bg_out, ng_out,
    xs, ks, cs, w, kown, wg, gst, hhalf, hleft, hright, hcross, ghalf, gleft, gright, gcross,
    vblk, acc, yout, cols, stat, fin, rowt, colg, bsum, pack, land,
    loc_sem, wg_sem,
    c_ss, c_rs, x_ss, x_rs, k_ss, k_rs, h_ss, h_rs, g_ss, g_rs,
    stat_ss, stat_rs, fin_ss, fin_rs, rowt_ss, rowt_rs, colg_ss, colg_rs, a_ss, a_rs,
):
    section = lax.axis_index("section")
    dp, mp = Spot("dp"), Spot("mp")
    rows, width = fwd.shape
    full = width * GROUP
    n_blocks = width // MXU

    loads = [
        pltpu.make_async_copy(cot, cs.at[mp.index], loc_sem.at[0]),
        pltpu.make_async_copy(fwd, xs.at[dp.index], loc_sem.at[1]),
        pltpu.make_async_copy(kept, ks.at[dp.index], loc_sem.at[2]),
        pltpu.make_async_copy(kept, kown, loc_sem.at[3]),
        pltpu.make_async_copy(weight, w, loc_sem.at[4]),
    ]
    for load in loads:
        load.start()

    barrier = pltpu.get_barrier_semaphore()
    for spot in (mp, dp):
        for step in range(1, GROUP):
            pl.semaphore_signal(
                barrier, inc=1, device_id={spot.group: lax.rem(spot.index + step, GROUP)}, device_id_type=MESH
            )

    def greet(i, carry):
        pl.semaphore_signal(
            barrier,
            inc=1,
            device_id={"section": 1 - section, "dp": lax.div(i, GROUP), "mp": lax.rem(i, GROUP)},
            device_id_type=MESH,
        )
        return carry

    lax.fori_loop(0, GROUP * GROUP, greet, 0)
    pl.semaphore_wait(barrier, 2 * (GROUP - 1) + GROUP * GROUP)

    gc = Gather(mp, cs, c_ss, c_rs, False)
    gx = Gather(dp, xs, x_ss, x_rs, True)
    gk = Gather(dp, ks, k_ss, k_rs, True)
    loads[0].wait()
    for c in (0, 1):
        for kind in (0, 1, 2):
            gc.start(kind, c)
    loads[1].wait()
    for c in (0, 1):
        for kind in (0, 1, 2):
            gx.start(kind, c)

    loads[2].wait()
    lane = lax.broadcasted_iota(jnp.int32, (TILE, 128), 1)

    def in_lanes(values):
        result = jnp.zeros((TILE, 128), F32)
        for i, value in enumerate(values):
            result = jnp.where(lane == i, value, result)
        return result

    def row_sums(at):
        x = xs[dp.index, at].astype(F32)
        k = ks[dp.index, at].astype(F32)
        sums = [jnp.sum(v, 1, keepdims=True) for v in (x, x * x, k, k * k)]
        cols[at] = in_lanes(sums)

    tiles(rows, row_sums)
    stats = Spread(mp, stat, stat_ss, stat_rs)
    stat[mp.index] = jnp.transpose(cols[...])[0:8]
    stats.start()
    stats.arrived()
    sums = stats.total() / full
    mean_x, mean_k = sums[0:1], sums[2:3]
    inv_x = lax.rsqrt(sums[1:2] - mean_x * mean_x + EPS)
    inv_k = lax.rsqrt(sums[3:4] - mean_k * mean_k + EPS)
    row = lax.broadcasted_iota(jnp.int32, (8, rows), 0)
    fin[dp.index] = jnp.where(row == 0, mean_x, jnp.where(row == 1, inv_x, jnp.where(row == 2, mean_k, inv_k)))
    finished = Spread(dp, fin, fin_ss, fin_rs)
    finished.start()

    def forward(gather):
        gather.arrived(1, 0)
        gather.start(5, 0)
        gather.arrived(2, 1)
        gather.start(5, 1)

    forward(gc)
    forward(gx)
    for c in (0, 1):
        for gather in (gc, gx):
            gather.arrived(0, c)
            gather.start(3, c)
            gather.start(4, c)
    for c in (0, 1):
        gx.arrived(5, c)
        gx.start(6, c)
    gc.arrived(3, 0)
    gc.start(6, 0)
    gc.arrived(4, 1)
    gc.start(6, 1)
    for c in (0, 1):
        gk.start(1, c)
        gk.start(2, c)
    for kind, c in ((1, 1), (2, 0), (3, 0), (3, 1), (4, 0), (4, 1), (6, 0), (6, 1)):
        gx.arrived(kind, c)
    finished.arrived()
    loads[4].wait()
    gx.finish()
    for kind, c in ((1, 1), (2, 0), (3, 1), (4, 0), (5, 0), (5, 1), (6, 0), (6, 1)):
        gc.arrived(kind, c)
    loads[3].wait()

    def normalise(buf, slot, out, which):
        cols[:, 0:8] = jnp.transpose(fin[slot])

        def body(at):
            mean = cols[at, which : which + 1]
            inv = cols[at, which + 1 : which + 2]
            hat = (buf[slot, at].astype(F32) - mean) * inv
            out[at] = (hat * gain[...] + shift[...]).astype(BF16)

        tiles(rows, body)

    bsum[...] = jnp.zeros_like(bsum)

    def product_h(slot):
        normalise(xs, slot, xs.at[slot], 0)

        def body(n, carry):
            at = pl.ds(pl.multiple_of(n * MXU, MXU), MXU)
            acc[:, at] = jnp.dot(xs[slot], w[:, at], preferred_element_type=F32)
            return carry

        lax.fori_loop(0, n_blocks, body, 0)

    def product_g(slot):
        def body(n, carry):
            at = pl.ds(pl.multiple_of(n * MXU, MXU), MXU)
            acc[:, at] = lax.dot_general(
                cs[slot], w[at, :], (((1,), (1,)), ((), ())), preferred_element_type=F32
            )
            return carry

        lax.fori_loop(0, n_blocks, body, 0)

        def add(at):
            c = cs[slot, at].astype(F32)
            bsum[...] += c[0:8] + c[8:16]

        tiles(rows, add)

    half = rows // 2

    def emit(stage, start, terms):
        def body(i, carry):
            at = pl.ds(pl.multiple_of(start + i * TILE, TILE), TILE)
            value = acc[at]
            for term in terms:
                value = value + term[at].astype(F32)
            stage[at] = value.astype(BF16)
            return carry

        lax.fori_loop(0, half // TILE, body, 0)

    def stage_g(side, ring_step):
        place = {2: 0, 1: 1, -1: 2, 0: 3}[ring_step] * 2 + side
        return gst.at[place]

    def stage_h(side, ring_step):
        return xs.at[mp.slot(1 - side, ring_step)]

    rg = Scatter(dp, stage_g, ghalf, gleft, gright, gcross, g_ss, g_rs)
    rh = Scatter(mp, stage_h, hhalf, hleft, hright, hcross, h_ss, h_rs)
    work = ((rg, product_g), (rh, product_h))

    for side in (0, 1):
        for scatter, product in work:
            product(scatter.spot.slot(1 - side, 2))
            for c in (0, 1):
                emit(scatter.stage(side, 2), c * half, [])
                scatter.start(0, side, c)
    for c in (0, 1):
        gk.start(0, c)
    for side in (0, 1):
        for scatter, product in work:
            product(scatter.spot.slot(1 - side, 1))
            emit(scatter.stage(side, 1), half, [])
            scatter.start(1, side, 1)
            scatter.arrived(0, side, 0)
            emit(scatter.stage(side, 1), 0, [scatter.halves.at[side]])
            scatter.start(1, side, 0)
            product(scatter.spot.slot(1 - side, -1))
            emit(scatter.stage(side, -1), 0, [])
            scatter.start(2, side, 0)
            scatter.arrived(0, side, 1)
            emit(scatter.stage(side, -1), half, [scatter.halves.at[side]])
            scatter.start(2, side, 1)
    forward(gk)
    for c in (0, 1):
        gk.arrived(0, c)
        gk.start(3, c)
        gk.start(4, c)
    for scatter, product in work:
        product(scatter.spot.slot(1, 0))
        for c in (0, 1):
            scatter.arrived(1, 0, c)
            scatter.arrived(2, 0, c)
            emit(scatter.stage(0, 0), c * half, [scatter.left.at[0], scatter.right.at[0]])
            scatter.start(3, 0, c)
    for c in (0, 1):
        gk.arrived(5, c)
        gk.start(6, c)

    def whole(scatter, finish):
        for c in (0, 1):
            for kind, side in ((1, 1), (2, 1), (3, 0)):
                scatter.arrived(kind, side, c)

        def body(at):
            value = acc[at]
            for term in (scatter.left.at[1], scatter.right.at[1], scatter.crossed):
                value = value + term[at].astype(F32)
            finish(at, value)

        tiles(rows, body)

    def finish_h(at, value):
        yout[at] = (value + bias[...]).astype(BF16)

    product_h(mp.slot(0, 0))
    whole(rh, finish_h)

    product_g(dp.slot(0, 0))
    cols[:, 0:8] = jnp.transpose(fin[dp.index])
    colg[dp.index] = jnp.zeros(colg.shape[1:], F32)

    def hat_kept(at):
        return (kown[at].astype(F32) - cols[at, 2:3]) * cols[at, 3:4]

    def finish_g(at, value):
        hat = hat_kept(at)
        colg[dp.index, 0:1] += jnp.sum(value * hat, 0, keepdims=True)
        colg[dp.index, 1:2] += jnp.sum(value, 0, keepdims=True)
        acc[at] = value
        scaled = value * gain[...]
        terms = [jnp.sum(v, 1, keepdims=True) for v in (scaled, scaled * hat)]
        lanes = in_lanes([terms[0], terms[1]])
        cols[at, 8:16] = lanes[:, 0:8]

    whole(rg, finish_g)
    column = Spread(dp, colg, colg_ss, colg_rs)
    column.start()
    terms = Spread(mp, rowt, rowt_ss, rowt_rs)
    rowt[mp.index] = jnp.transpose(cols[...])[8:16]
    terms.start()
    terms.arrived()
    cols[:, 8:16] = jnp.transpose(terms.total() / full)

    def input_grad(at):
        hat = hat_kept(at)
        scaled = acc[at] * gain[...]
        grad = cols[at, 3:4] * (scaled - cols[at, 8:9] - hat * cols[at, 9:10])
        acc[at] = grad

    tiles(rows, input_grad)

    piece_rows, piece_cols = pack.shape[2:]

    def packing(b, carry):
        at = pl.ds(pl.multiple_of(b * piece_rows, piece_rows), piece_rows)
        out = yout[at].astype(F32)
        grad = acc[at]
        sent = jnp.where(section == 0, out, grad)
        yout[at] = jnp.where(section == 0, grad, out).astype(BF16)
        for f in range(GROUP):
            pack[b, f] = sent[:, f * piece_cols : (f + 1) * piece_cols].astype(BF16)
        return carry

    lax.fori_loop(0, GROUP, packing, 0)
    first = section == 0
    row_at = jnp.where(first, mp.index, dp.index)
    col_at = jnp.where(first, dp.index, mp.index)

    def piece(i):
        j = lax.rem(i + dp.index * GROUP + mp.index, GROUP * GROUP)
        b, f = lax.div(j, GROUP), lax.rem(j, GROUP)
        return pltpu.make_async_remote_copy(
            src_ref=pack.at[b, f],
            dst_ref=land.at[row_at, col_at],
            send_sem=a_ss.at[j],
            recv_sem=a_rs.at[row_at * GROUP + col_at],
            device_id={"section": 1 - section, "dp": jnp.where(first, b, f), "mp": jnp.where(first, f, b)},
            device_id_type=MESH,
        )

    def send_piece(i, carry):
        piece(i).start()
        return carry

    lax.fori_loop(0, GROUP * GROUP, send_piece, 0)
    keep = pltpu.make_async_copy(yout, passed_out, loc_sem.at[0])
    keep.start()

    wg[...] = jnp.zeros_like(wg)

    def product_w(slot):
        normalise(ks, slot, vblk, 2)

        def body(n, carry):
            at = pl.ds(pl.multiple_of(n * MXU, MXU), MXU)
            wg[at, :] += lax.dot_general(
                vblk[:, at], cs[slot], (((0,), (0,)), ((), ())), preferred_element_type=F32
            )
            return carry

        lax.fori_loop(0, n_blocks, body, 0)

    for kind, c in ((1, 1), (2, 0)):
        gk.arrived(kind, c)
    for pair_step, ring_step, kinds in (
        (0, 0, ()), (1, 0, ()), (0, 1, ()), (0, -1, ()), (0, 2, ()), (1, 1, (4,)), (1, -1, (3,)), (1, 2, (6,))
    ):
        for kind in kinds:
            for c in (0, 1):
                gk.arrived(kind, c)
        product_w(dp.slot(pair_step, ring_step))
    store = pltpu.make_async_copy(wg, wg_out, wg_sem)
    store.start()

    bg_out[...] = jnp.sum(bsum[...], 0, keepdims=True)
    column.arrived()
    ng_out[...] = column.total()

    def landed(i, carry):
        pltpu.make_async_remote_copy(
            src_ref=pack.at[0, 0],
            dst_ref=land.at[lax.div(i, GROUP), lax.rem(i, GROUP)],
            send_sem=a_ss.at[i],
            recv_sem=a_rs.at[i],
            device_id={"section": 1 - section},
            device_id_type=MESH,
        ).wait_recv()
        return carry

    lax.fori_loop(0, GROUP * GROUP, landed, 0)
    out = pltpu.make_async_copy(land, arrived_out, loc_sem.at[1])
    out.start()

    def left(i, carry):
        piece(i).wait_send()
        return carry

    lax.fori_loop(0, GROUP * GROUP, left, 0)
    for transfer in (gc, gk, rg, rh, stats, finished, column, terms):
        transfer.finish()
    keep.wait()
    store.wait()
    out.wait()


def shards(fwd_in, kept_in, cotangent, weight, bias, norm_gain, norm_shift):
    section_index = lax.axis_index("section")
    rows, cols = fwd_in.shape[3:]
    piece = (GROUP, GROUP, rows // GROUP, cols // GROUP)
    any_spec = pl.BlockSpec(memory_space=pl.ANY)
    vmem_spec = pl.BlockSpec(memory_space=pltpu.VMEM)
    dma = pltpu.SemaphoreType.DMA
    shard = pltpu.VMEM((rows, cols), BF16)
    gathered = pltpu.VMEM((GROUP, rows, cols), BF16)
    two = pltpu.VMEM((2, rows, cols), BF16)
    arrived, passed, weight_grad, bias_grad, norm_grads = pl.pallas_call(
        relay_kernel,
        name="relay",
        out_shape=(
            jax.ShapeDtypeStruct(piece, BF16),
            jax.ShapeDtypeStruct((rows, cols), BF16),
            jax.ShapeDtypeStruct((cols, cols), F32),
            jax.ShapeDtypeStruct((1, cols), F32),
            jax.ShapeDtypeStruct((2, cols), F32),
        ),
        in_specs=[any_spec] * 4 + [vmem_spec] * 3,
        out_specs=(any_spec, any_spec, any_spec, vmem_spec, vmem_spec),
        scratch_shapes=[
            gathered, gathered, gathered, pltpu.VMEM((cols, cols), BF16), shard, pltpu.VMEM((cols, cols), F32),
            pltpu.VMEM((7, rows, cols), BF16),
            two, two, two, shard, two, two, two, shard,
            shard, pltpu.VMEM((rows, cols), F32), shard, pltpu.VMEM((rows, 128), F32),
            pltpu.VMEM((GROUP, 8, rows), F32), pltpu.VMEM((GROUP, 8, rows), F32), pltpu.VMEM((GROUP, 8, rows), F32),
            pltpu.VMEM((GROUP, 2, cols), F32), pltpu.VMEM((8, cols), F32),
            pltpu.VMEM(piece, BF16), pltpu.VMEM(piece, BF16),
            dma((5,)), dma,
            dma((7, 2)), dma((7, 2)), dma((7, 2)), dma((7, 2)), dma((7, 2)), dma((7, 2)),
            dma((16,)), dma((16,)), dma((16,)), dma((16,)),
            dma((7,)), dma((7,)), dma((7,)), dma((7,)), dma((7,)), dma((7,)), dma((7,)), dma((7,)),
            dma((GROUP * GROUP,)), dma((GROUP * GROUP,)),
        ],
        compiler_params=pltpu.CompilerParams(
            collective_id=0, has_side_effects=True, vmem_limit_bytes=60 * 2**20
        ),
    )(
        fwd_in.reshape(rows, cols),
        kept_in.reshape(rows, cols),
        cotangent.reshape(rows, cols),
        weight.reshape(cols, cols),
        bias.reshape(1, cols),
        norm_gain.reshape(1, cols),
        norm_shift.reshape(1, cols),
    )
    next_in = arrived.transpose(0, 2, 1, 3).reshape(fwd_in.shape)
    return (
        next_in,
        passed.reshape(fwd_in.shape),
        weight_grad.reshape(1, cols, cols),
        bias_grad,
        norm_grads.reshape(1, 2, cols),
    )


def solution(mesh):
    placed = (
        P("section", "dp", "mp", None, None),
        P("section", "dp", "mp", None, None),
        P("section", "dp", "mp", None, None),
        P("section", "mp", "dp"),
        P("section", "dp"),
        P("section", "mp"),
        P("section", "mp"),
    )
    return jax.shard_map(
        shards,
        mesh=mesh,
        in_specs=placed,
        out_specs=(
            P("section", "dp", "mp", None, None),
            P("section", "dp", "mp", None, None),
            P("section", "mp", "dp"),
            P("section", "dp"),
            P("section", None, "mp"),
        ),
        check_vma=False,
    )
```

```python
import jax
import jax.numpy as jnp
from jax import lax
from jax.experimental import pallas as pl
from jax.experimental.pallas import tpu as pltpu
from jax.sharding import PartitionSpec as P

EPS = 1e-05
RING = 4
PAIR = 2
GROUP = RING * PAIR
TILE = 16
LATE = ((4, 1, 1), (3, 1, -1), (6, 1, 2))
MXU = 256
F32 = jnp.float32
BF16 = jnp.bfloat16
MESH = pl.DeviceIdType.MESH


class Spot:
    def __init__(self, group):
        self.group = group
        self.index = lax.axis_index(group)
        self.pair = lax.div(self.index, RING)
        self.ring = lax.rem(self.index, RING)

    def slot(self, pair_step, ring_step):
        pair = lax.rem(self.pair + pair_step, PAIR)
        return pair * RING + lax.rem(self.ring + ring_step + RING, RING)

    def device(self, pair_step, ring_step):
        return {self.group: self.slot(pair_step, ring_step)}


class Gather:
    def __init__(self, spot, buf, send_sem, recv_sem, far_by_pair):
        self.spot, self.buf, self.far_by_pair = spot, buf, far_by_pair
        self.send_sem, self.recv_sem = send_sem, recv_sem
        self.half = buf.shape[1] // 2
        self.started = []

    def route(self, kind, c):
        step = 1 if c == 0 else -1
        return {
            0: ((0, 0), (1, 0), (1, 0)),
            1: ((0, 0), (0, 1), (0, -1)),
            2: ((0, 0), (0, -1), (0, 1)),
            3: ((1, 0), (0, 1), (1, -1)),
            4: ((1, 0), (0, -1), (1, 1)),
            5: ((0, -step), (0, step), (0, 2)),
            6: ((0, 2), (1, 0), (1, 2)) if self.far_by_pair else ((1, -step), (0, step), (1, 2)),
        }[kind]

    def copy(self, kind, c, landing):
        source, target, lands = self.route(kind, c)
        here = self.spot.slot(*(lands if landing else source))
        view = self.buf.at[here, pl.ds(c * self.half, self.half)]
        return pltpu.make_async_remote_copy(
            src_ref=view,
            dst_ref=view,
            send_sem=self.send_sem.at[kind, c],
            recv_sem=self.recv_sem.at[kind, c],
            device_id=self.spot.device(*target),
            device_id_type=MESH,
        )

    def start(self, kind, c):
        self.copy(kind, c, False).start()
        self.started.append((kind, c))

    def arrived(self, kind, c):
        self.copy(kind, c, True).wait_recv()

    def sent(self, kind):
        for c in (0, 1):
            self.copy(kind, c, False).wait_send()
            self.started.remove((kind, c))

    def finish(self):
        for kind, c in self.started:
            self.copy(kind, c, False).wait_send()
        self.started = []


class Scatter:
    def __init__(self, spot, stage, halves, left, right, crossed, send_sem, recv_sem):
        self.spot, self.stage = spot, stage
        self.halves, self.left, self.right, self.crossed = halves, left, right, crossed
        self.send_sem, self.recv_sem = send_sem, recv_sem
        self.half = halves.shape[1] // 2
        self.started = []

    def copy(self, kind, side, c):
        spot, rows = self.spot, pl.ds(c * self.half, self.half)
        step = 1 if c == 0 else -1
        source, target, lands = {
            0: (self.stage(side, 2), (0, step), self.halves.at[side]),
            1: (self.stage(side, 1), (0, 1), self.left.at[side]),
            2: (self.stage(side, -1), (0, -1), self.right.at[side]),
            3: (self.stage(side, 0), (1, 0), self.crossed),
        }[kind]
        sem = (kind * 2 + side) * 2 + c
        return pltpu.make_async_remote_copy(
            src_ref=source.at[rows],
            dst_ref=lands.at[rows],
            send_sem=self.send_sem.at[sem],
            recv_sem=self.recv_sem.at[sem],
            device_id=spot.device(*target),
            device_id_type=MESH,
        )

    def start(self, kind, side, c):
        self.copy(kind, side, c).start()
        self.started.append((kind, side, c))

    def arrived(self, kind, side, c):
        self.copy(kind, side, c).wait_recv()

    def finish(self):
        for key in self.started:
            self.copy(*key).wait_send()
        self.started = []


class Spread:
    def __init__(self, spot, buf, send_sem, recv_sem):
        self.spot, self.buf, self.send_sem, self.recv_sem = spot, buf, send_sem, recv_sem

    def copy(self, step, landing):
        me = self.spot.index
        other = lax.rem(me + step, GROUP)
        view = self.buf.at[lax.rem(me + GROUP - step, GROUP) if landing else me]
        return pltpu.make_async_remote_copy(
            src_ref=view,
            dst_ref=view,
            send_sem=self.send_sem.at[step - 1],
            recv_sem=self.recv_sem.at[step - 1],
            device_id={self.spot.group: other},
            device_id_type=MESH,
        )

    def start(self):
        for step in range(1, GROUP):
            self.copy(step, False).start()

    def arrived(self):
        for step in range(1, GROUP):
            self.copy(step, True).wait_recv()

    def finish(self):
        for step in range(1, GROUP):
            self.copy(step, False).wait_send()

    def total(self):
        result = self.buf[0]
        for i in range(1, GROUP):
            result = result + self.buf[i]
        return result


def tiles(count, body, size=TILE):
    def step(i, carry):
        body(pl.ds(pl.multiple_of(i * size, size), size))
        return carry

    lax.fori_loop(0, count // size, step, 0, unroll=4)


def relay_kernel(
    fwd, kept, cot, weight, bias, gain, shift,
    arrived_out, passed_out, wg_out, v_out, c_out, bg_out, ng_out,
    xs, ks, cs, w, kown, wg, gst, hhalf, hleft, hright, hcross, ghalf, gleft, gright, gcross,
    vblk, acc, accg, yout, cols, stat, fin, rowt, colg, bsum, pack, land,
    loc_sem, wg_sem, late_sem,
    c_ss, c_rs, x_ss, x_rs, k_ss, k_rs, h_ss, h_rs, g_ss, g_rs,
    stat_ss, stat_rs, fin_ss, fin_rs, rowt_ss, rowt_rs, colg_ss, colg_rs, a_ss, a_rs,
):
    section = lax.axis_index("section")
    dp, mp = Spot("dp"), Spot("mp")
    rows, width = fwd.shape
    full = width * GROUP
    wide = width // 2

    loads = [
        pltpu.make_async_copy(cot, cs.at[mp.index], loc_sem.at[0]),
        pltpu.make_async_copy(fwd, xs.at[dp.index], loc_sem.at[1]),
        pltpu.make_async_copy(kept, ks.at[dp.index], loc_sem.at[2]),
        pltpu.make_async_copy(kept, kown, loc_sem.at[3]),
        pltpu.make_async_copy(weight, w, loc_sem.at[4]),
    ]
    for i in (1, 2, 0):
        loads[i].start()

    barrier = pltpu.get_barrier_semaphore()
    for spot in (mp, dp):
        for step in range(1, GROUP):
            pl.semaphore_signal(
                barrier, inc=1, device_id={spot.group: lax.rem(spot.index + step, GROUP)}, device_id_type=MESH
            )

    pl.semaphore_signal(barrier, inc=1, device_id={"section": 1 - section}, device_id_type=MESH)

    lane = lax.broadcasted_iota(jnp.int32, (TILE, 128), 1)

    def in_lanes(values):
        result = jnp.zeros((TILE, 128), F32)
        for i, value in enumerate(values):
            result = jnp.where(lane == i, value, result)
        return result

    def row_sums(at):
        x = xs[dp.index, at].astype(F32)
        k = ks[dp.index, at].astype(F32)
        sums = [jnp.sum(v, 1, keepdims=True) for v in (x, x * x, k, k * k)]
        cols[at] = in_lanes(sums)

    loads[1].wait()
    loads[2].wait()
    tiles(rows, row_sums)
    stat[mp.index] = jnp.transpose(cols[...])[0:8]
    loads[0].wait()
    pl.semaphore_wait(barrier, 2 * (GROUP - 1) + 1)

    gc = Gather(mp, cs, c_ss, c_rs, False)
    gx = Gather(dp, xs, x_ss, x_rs, True)
    gk = Gather(dp, ks, k_ss, k_rs, True)
    stats = Spread(mp, stat, stat_ss, stat_rs)
    stats.start()
    for c in (0, 1):
        for gather in (gc, gx):
            gather.start(0, c)
            gather.start(1, c)
            gather.start(2, 1 - c)
    loads[4].start()
    loads[3].start()
    stats.arrived()
    sums = stats.total() / full
    mean_x, mean_k = sums[0:1], sums[2:3]
    inv_x = lax.rsqrt(sums[1:2] - mean_x * mean_x + EPS)
    inv_k = lax.rsqrt(sums[3:4] - mean_k * mean_k + EPS)
    row = lax.broadcasted_iota(jnp.int32, (8, rows), 0)
    fin[dp.index] = jnp.where(row == 0, mean_x, jnp.where(row == 1, inv_x, jnp.where(row == 2, mean_k, inv_k)))
    finished = Spread(dp, fin, fin_ss, fin_rs)
    finished.start()

    def forward(gather):
        gather.arrived(1, 0)
        gather.start(5, 0)
        gather.arrived(2, 1)
        gather.start(5, 1)

    for gather in (gc, gx):
        forward(gather)
    for c in (0, 1):
        for gather in (gc, gx):
            gather.arrived(0, c)
            gather.start(3, c)
            gather.start(4, c)
        if c == 0:
            for d in (0, 1):
                gx.arrived(5, d)
                gx.start(6, d)
    gk.start(1, 0)
    gk.start(2, 1)
    gc.arrived(3, 0)
    gc.start(6, 0)
    gc.arrived(4, 1)
    gc.start(6, 1)

    def normalise(buf, slot, out, which):
        cols[:, 0:8] = jnp.transpose(fin[slot])

        def body(at):
            mean = cols[at, which : which + 1]
            inv = cols[at, which + 1 : which + 2]
            hat = (buf[slot, at].astype(F32) - mean) * inv
            out[at] = (hat * gain[...] + shift[...]).astype(BF16)

        tiles(rows, body)

    finished.arrived()
    for steps, kinds, sent in (
        ((0, 0), (), (0, 1, 2)),
        ((0, 1), ((2, 0),), (5,)),
        ((0, -1), ((1, 1),), ()),
        ((1, 0), (), (3, 4)),
        ((1, 1), ((4, 0), (4, 1)), ()),
        ((1, -1), ((3, 0), (3, 1)), ()),
        ((0, 2), (), (6,)),
        ((1, 2), ((6, 0), (6, 1)), ()),
    ):
        for key in kinds:
            gx.arrived(*key)
        for kind in sent:
            gx.sent(kind)
        slot = dp.slot(*steps)
        normalise(xs, slot, xs.at[slot], 0)
    loads[4].wait()
    for kind, c in ((1, 1), (2, 0), (3, 1), (4, 0), (5, 0), (5, 1), (6, 0), (6, 1)):
        gc.arrived(kind, c)
    loads[3].wait()

    def product_h(slot, acc):
        def body(n, carry):
            at = pl.ds(pl.multiple_of(n * wide, MXU), wide)
            acc[:, at] = jnp.dot(xs[slot], w[:, at], preferred_element_type=F32)
            return carry

        lax.fori_loop(0, width // wide, body, 0)

    def product_g(slot, acc):
        def body(n, carry):
            at = pl.ds(pl.multiple_of(n * wide, MXU), wide)
            acc[:, at] = lax.dot_general(
                cs[slot], w[at, :], (((1,), (1,)), ((), ())), preferred_element_type=F32
            )
            return carry

        lax.fori_loop(0, width // wide, body, 0)

    def product_w(pair_step, ring_step, fresh=False):
        slot = dp.slot(pair_step, ring_step)
        normalise(ks, slot, vblk, 2)

        def body(n, carry):
            at = pl.ds(pl.multiple_of(n * wide, MXU), wide)
            term = lax.dot_general(
                vblk[:, at], cs[slot], (((0,), (0,)), ((), ())), preferred_element_type=F32
            )
            wg[at, :] = term if fresh else wg[at, :] + term
            return carry

        lax.fori_loop(0, width // wide, body, 0)

    def late(i):
        slot, to = dp.slot(*LATE[i][1:]), pl.ds(i * rows, rows)
        return (
            pltpu.make_async_copy(ks.at[slot], v_out.at[to], late_sem.at[2 * i]),
            pltpu.make_async_copy(cs.at[slot], c_out.at[to], late_sem.at[2 * i + 1]),
        )

    half = rows // 2

    def emit(stage, start, terms, acc):
        def body(i, carry):
            at = pl.ds(pl.multiple_of(start + i * TILE, TILE), TILE)
            value = acc[at]
            for term in terms:
                value = value + term[at].astype(F32)
            stage[at] = value.astype(BF16)
            return carry

        lax.fori_loop(0, half // TILE, body, 0, unroll=4)

    def stage_g(side, ring_step):
        place = {2: 0, 1: 1, -1: 2, 0: 3}[ring_step] * 2 + side
        return gst.at[place]

    def stage_h(side, ring_step):
        return xs.at[mp.slot(1 - side, ring_step)]

    rg = Scatter(dp, stage_g, ghalf, gleft, gright, gcross, g_ss, g_rs)
    rh = Scatter(mp, stage_h, hhalf, hleft, hright, hcross, h_ss, h_rs)
    work_g, work_h = (rg, product_g), (rh, product_h)

    def far(scatter, product, side):
        product(scatter.spot.slot(1 - side, 2), acc)
        for c in (0, 1):
            emit(scatter.stage(side, 2), c * half, [], acc)
            scatter.start(0, side, c)

    def near(scatter, product, side):
        product(scatter.spot.slot(1 - side, 1), acc)
        scatter.arrived(0, side, 0)
        for c in (0, 1):
            emit(scatter.stage(side, 1), c * half, [] if c else [scatter.halves.at[side]], acc)
            scatter.start(1, side, c)
        product(scatter.spot.slot(1 - side, -1), acc)
        for c in (0, 1):
            if c:
                scatter.arrived(0, side, 1)
            emit(scatter.stage(side, -1), c * half, [scatter.halves.at[side]] if c else [], acc)
            scatter.start(2, side, c)

    def cross(scatter, c, acc):
        scatter.arrived(1, 0, c)
        scatter.arrived(2, 0, c)
        emit(scatter.stage(0, 0), c * half, [scatter.left.at[0], scatter.right.at[0]], acc)
        scatter.start(3, 0, c)

    far(*work_g, 0)
    far(*work_h, 0)
    for c in (0, 1):
        gk.start(0, c)
    near(*work_g, 0)
    near(*work_h, 0)
    far(*work_g, 1)
    far(*work_h, 1)
    product_g(dp.slot(1, 0), accg)
    cross(rg, 0, accg)
    near(*work_g, 1)
    near(*work_h, 1)
    cross(rg, 1, accg)
    product_h(mp.slot(1, 0), accg)
    cross(rh, 0, accg)
    cross(rh, 1, accg)
    gk.start(1, 1)
    gk.start(2, 0)
    forward(gk)
    for c in (0, 1):
        gk.arrived(0, c)
        gk.start(3, c)
        gk.start(4, c)

    bsum[...] = jnp.zeros_like(bsum)

    def add_block(slot, carry):
        def add(at):
            c = cs[slot, at].astype(F32)
            bsum[...] += c[0:8] + c[8:16]

        tiles(rows, add)
        return carry

    lax.fori_loop(0, GROUP, add_block, 0)
    product_w(0, 0, True)
    product_w(1, 0)

    def whole(scatter, acc, finish):
        for c in (0, 1):
            for kind, side in ((1, 1), (2, 1), (3, 0)):
                scatter.arrived(kind, side, c)

        def body(at):
            value = acc[at]
            for term in (scatter.left.at[1], scatter.right.at[1], scatter.crossed):
                value = value + term[at].astype(F32)
            finish(at, value)

        tiles(rows, body)

    def hat_kept(at):
        return (kown[at].astype(F32) - cols[at, 2:3]) * cols[at, 3:4]

    def finish_g(at, value):
        hat = hat_kept(at)
        colg[dp.index, 0:1] += jnp.sum(value * hat, 0, keepdims=True)
        colg[dp.index, 1:2] += jnp.sum(value, 0, keepdims=True)
        accg[at] = value
        scaled = value * gain[...]
        terms = [jnp.sum(v, 1, keepdims=True) for v in (scaled, scaled * hat)]
        lanes = in_lanes(terms)
        cols[at, 8:16] = lanes[:, 0:8]

    product_g(dp.slot(0, 0), accg)
    product_h(mp.slot(0, 0), acc)
    cols[:, 0:8] = jnp.transpose(fin[dp.index])
    colg[dp.index] = jnp.zeros(colg.shape[1:], F32)
    whole(rg, accg, finish_g)
    terms = Spread(mp, rowt, rowt_ss, rowt_rs)
    rowt[mp.index] = jnp.transpose(cols[...])[8:16]
    terms.start()
    column = Spread(dp, colg, colg_ss, colg_rs)
    column.start()

    piece_rows, piece_cols = pack.shape[2:]
    first = section == 0
    row_at = jnp.where(first, mp.index, dp.index)
    col_at = jnp.where(first, dp.index, mp.index)

    def piece(i):
        j = lax.rem(i + dp.index * GROUP + mp.index, GROUP * GROUP)
        b, f = lax.div(j, GROUP), lax.rem(j, GROUP)
        return pltpu.make_async_remote_copy(
            src_ref=pack.at[b, f],
            dst_ref=land.at[row_at, col_at],
            send_sem=a_ss.at[j],
            recv_sem=a_rs.at[row_at * GROUP + col_at],
            device_id={"section": 1 - section, "dp": jnp.where(first, b, f), "mp": jnp.where(first, f, b)},
            device_id_type=MESH,
        )

    def send_piece(i, carry):
        piece(i).start()
        return carry

    def relay(values):
        def packing(b, carry):
            at = pl.ds(pl.multiple_of(b * piece_rows, piece_rows), piece_rows)
            sent = values[at]
            for f in range(GROUP):
                pack[b, f] = sent[:, f * piece_cols : (f + 1) * piece_cols].astype(BF16)
            return carry

        lax.fori_loop(0, GROUP, packing, 0)
        lax.fori_loop(0, GROUP * GROUP, send_piece, 0)

    def finish_h(at, value):
        acc[at] = value + bias[...]

    whole(rh, acc, finish_h)

    @pl.when(first)
    def _():
        relay(acc)

    terms.arrived()
    cols[:, 8:16] = jnp.transpose(terms.total() / full)

    def input_grad(at):
        hat = hat_kept(at)
        scaled = accg[at] * gain[...]
        accg[at] = cols[at, 3:4] * (scaled - cols[at, 8:9] - hat * cols[at, 9:10])

    tiles(rows, input_grad)

    @pl.when(section == 1)
    def _():
        relay(accg)

    def keeping(at):
        yout[at] = jnp.where(first, accg[at], acc[at]).astype(BF16)

    tiles(rows, keeping)
    keep = pltpu.make_async_copy(yout, passed_out, loc_sem.at[0])
    keep.start()

    gk.arrived(1, 1)
    gk.arrived(2, 0)
    product_w(0, 1)
    product_w(0, -1)
    for c in (0, 1):
        gk.arrived(5, c)
        gk.start(6, c)
    product_w(0, 2)
    store = pltpu.make_async_copy(wg, wg_out, wg_sem)
    store.start()
    for i in range(len(LATE)):
        late(i)[1].start()
    for i, (kind, pair_step, ring_step) in enumerate(LATE):
        for c in (0, 1):
            gk.arrived(kind, c)
        slot = dp.slot(pair_step, ring_step)
        normalise(ks, slot, ks.at[slot], 2)
        late(i)[0].start()

    bg_out[...] = jnp.sum(bsum[...], 0, keepdims=True)
    column.arrived()
    ng_out[...] = column.total()

    def landed(i, carry):
        pltpu.make_async_remote_copy(
            src_ref=pack.at[0, 0],
            dst_ref=land.at[lax.div(i, GROUP), lax.rem(i, GROUP)],
            send_sem=a_ss.at[i],
            recv_sem=a_rs.at[i],
            device_id={"section": 1 - section},
            device_id_type=MESH,
        ).wait_recv()
        return carry

    lax.fori_loop(0, GROUP * GROUP, landed, 0)
    out = pltpu.make_async_copy(land, arrived_out, loc_sem.at[1])
    out.start()

    def left(i, carry):
        piece(i).wait_send()
        return carry

    lax.fori_loop(0, GROUP * GROUP, left, 0)
    for transfer in (gc, gk, rg, rh, stats, finished, column, terms):
        transfer.finish()
    keep.wait()
    store.wait()
    for i in range(len(LATE)):
        for copy in late(i):
            copy.wait()
    out.wait()


def finish_kernel(
    arrived, passed, early, late_v, late_c, bias_grad, norm_grads, next_out, passed_out, wg_out, bg_out, ng_out
):
    wg_out[...] = early[...] + lax.dot_general(
        late_v[...], late_c[...], (((0,), (0,)), ((), ())), preferred_element_type=F32
    )

    @pl.when(pl.program_id(0) == 0)
    def _():
        piece_rows = arrived.shape[2]

        def body(a, carry):
            row = jnp.concatenate([arrived[a, e].astype(F32) for e in range(GROUP)], axis=1)
            next_out[pl.ds(pl.multiple_of(a * piece_rows, piece_rows), piece_rows)] = row.astype(BF16)
            return carry

        lax.fori_loop(0, GROUP, body, 0)
        passed_out[...] = passed[...]
        bg_out[...] = bias_grad[...]
        ng_out[...] = norm_grads[...]


def shards(fwd_in, kept_in, cotangent, weight, bias, norm_gain, norm_shift):
    section_index = lax.axis_index("section")
    rows, cols = fwd_in.shape[3:]
    piece = (GROUP, GROUP, rows // GROUP, cols // GROUP)
    any_spec = pl.BlockSpec(memory_space=pl.ANY)
    vmem_spec = pl.BlockSpec(memory_space=pltpu.VMEM)
    dma = pltpu.SemaphoreType.DMA
    shard = pltpu.VMEM((rows, cols), BF16)
    gathered = pltpu.VMEM((GROUP, rows, cols), BF16)
    two = pltpu.VMEM((2, rows, cols), BF16)
    arrived, passed, early, late_v, late_c, bias_grad, norm_grads = pl.pallas_call(
        relay_kernel,
        name="relay",
        out_shape=(
            jax.ShapeDtypeStruct(piece, BF16),
            jax.ShapeDtypeStruct((rows, cols), BF16),
            jax.ShapeDtypeStruct((cols, cols), F32),
            jax.ShapeDtypeStruct((len(LATE) * rows, cols), BF16),
            jax.ShapeDtypeStruct((len(LATE) * rows, cols), BF16),
            jax.ShapeDtypeStruct((1, cols), F32),
            jax.ShapeDtypeStruct((2, cols), F32),
        ),
        in_specs=[any_spec] * 4 + [vmem_spec] * 3,
        out_specs=(any_spec,) * 5 + (vmem_spec,) * 2,
        scratch_shapes=[
            gathered, gathered, gathered, pltpu.VMEM((cols, cols), BF16), shard, pltpu.VMEM((cols, cols), F32),
            pltpu.VMEM((7, rows, cols), BF16),
            two, two, two, shard, two, two, two, shard,
            shard, pltpu.VMEM((rows, cols), F32), pltpu.VMEM((rows, cols), F32), shard, pltpu.VMEM((rows, 128), F32),
            pltpu.VMEM((GROUP, 8, rows), F32), pltpu.VMEM((GROUP, 8, rows), F32), pltpu.VMEM((GROUP, 8, rows), F32),
            pltpu.VMEM((GROUP, 2, cols), F32), pltpu.VMEM((8, cols), F32),
            pltpu.VMEM(piece, BF16), pltpu.VMEM(piece, BF16),
            dma((5,)), dma, dma((2 * len(LATE),)),
            dma((7, 2)), dma((7, 2)), dma((7, 2)), dma((7, 2)), dma((7, 2)), dma((7, 2)),
            dma((16,)), dma((16,)), dma((16,)), dma((16,)),
            dma((7,)), dma((7,)), dma((7,)), dma((7,)), dma((7,)), dma((7,)), dma((7,)), dma((7,)),
            dma((GROUP * GROUP,)), dma((GROUP * GROUP,)),
        ],
        compiler_params=pltpu.CompilerParams(
            collective_id=0, has_side_effects=True, vmem_limit_bytes=60 * 2**20
        ),
    )(
        fwd_in.reshape(rows, cols),
        kept_in.reshape(rows, cols),
        cotangent.reshape(rows, cols),
        weight.reshape(cols, cols),
        bias.reshape(1, cols),
        norm_gain.reshape(1, cols),
        norm_shift.reshape(1, cols),
    )
    fixed = lambda *shape: pl.BlockSpec(shape, lambda i: (0,) * len(shape))
    tile = pl.BlockSpec((MXU, cols), lambda i: (i, 0))
    next_in, passed, weight_grad, bias_grad, norm_grads = pl.pallas_call(
        finish_kernel,
        name="finish",
        grid=(cols // MXU,),
        out_shape=(
            jax.ShapeDtypeStruct((rows, cols), BF16),
            jax.ShapeDtypeStruct((rows, cols), BF16),
            jax.ShapeDtypeStruct((cols, cols), F32),
            jax.ShapeDtypeStruct((1, cols), F32),
            jax.ShapeDtypeStruct((2, cols), F32),
        ),
        in_specs=[
            fixed(*piece),
            fixed(rows, cols),
            tile,
            pl.BlockSpec((len(LATE) * rows, MXU), lambda i: (0, i)),
            fixed(len(LATE) * rows, cols),
            fixed(1, cols),
            fixed(2, cols),
        ],
        out_specs=(fixed(rows, cols), fixed(rows, cols), tile, fixed(1, cols), fixed(2, cols)),
        compiler_params=pltpu.CompilerParams(vmem_limit_bytes=60 * 2**20),
    )(arrived, passed, early, late_v, late_c, bias_grad, norm_grads)
    return (
        next_in.reshape(fwd_in.shape),
        passed.reshape(fwd_in.shape),
        weight_grad.reshape(1, cols, cols),
        bias_grad,
        norm_grads.reshape(1, 2, cols),
    )


def solution(mesh):
    placed = (
        P("section", "dp", "mp", None, None),
        P("section", "dp", "mp", None, None),
        P("section", "dp", "mp", None, None),
        P("section", "mp", "dp"),
        P("section", "dp"),
        P("section", "mp"),
        P("section", "mp"),
    )
    return jax.shard_map(
        shards,
        mesh=mesh,
        in_specs=placed,
        out_specs=(
            P("section", "dp", "mp", None, None),
            P("section", "dp", "mp", None, None),
            P("section", "mp", "dp"),
            P("section", "dp"),
            P("section", None, "mp"),
        ),
        check_vma=False,
    )
```

```python
import jax
import jax.numpy as jnp
from jax import lax
from jax.experimental import pallas as pl
from jax.experimental.pallas import tpu as pltpu
from jax.sharding import PartitionSpec as P

EPS = 1e-05
RING = 4
PAIR = 2
GROUP = RING * PAIR
TILE = 16
MXU = 256
LANES = 128
F32 = jnp.float32
BF16 = jnp.bfloat16
MESH = pl.DeviceIdType.MESH


class Spot:
    def __init__(self, group):
        self.group = group
        self.index = lax.axis_index(group)
        self.pair = lax.div(self.index, RING)
        self.ring = lax.rem(self.index, RING)

    def slot(self, pair_step, ring_step):
        pair = lax.rem(self.pair + pair_step, PAIR)
        return pair * RING + lax.rem(self.ring + ring_step + RING, RING)

    def device(self, pair_step, ring_step):
        return {self.group: self.slot(pair_step, ring_step)}


class Gather:
    def __init__(self, spot, buf, send_sem, recv_sem, far_by_pair, parts=2):
        self.spot, self.buf, self.far_by_pair, self.parts = spot, buf, far_by_pair, parts
        self.send_sem, self.recv_sem = send_sem, recv_sem
        self.part = buf.shape[1] // parts
        self.started = []

    def route(self, kind, c):
        step = 1 if c < self.parts // 2 else -1
        return {
            0: ((0, 0), (1, 0), (1, 0)),
            1: ((0, 0), (0, 1), (0, -1)),
            2: ((0, 0), (0, -1), (0, 1)),
            3: ((1, 0), (0, 1), (1, -1)),
            4: ((1, 0), (0, -1), (1, 1)),
            5: ((0, -step), (0, step), (0, 2)),
            7: ((0, -1), (1, 0), (1, -1)),
            8: ((0, 1), (1, 0), (1, 1)),
            6: ((0, 2), (1, 0), (1, 2)) if self.far_by_pair else ((1, -step), (0, step), (1, 2)),
        }[kind]

    def copy(self, kind, c, landing):
        source, target, lands = self.route(kind, c)
        here = self.spot.slot(*(lands if landing else source))
        view = self.buf.at[here, pl.ds(c * self.part, self.part)]
        return pltpu.make_async_remote_copy(
            src_ref=view,
            dst_ref=view,
            send_sem=self.send_sem.at[kind, c],
            recv_sem=self.recv_sem.at[kind, c],
            device_id=self.spot.device(*target),
            device_id_type=MESH,
        )

    def start(self, kind, c):
        self.copy(kind, c, False).start()
        self.started.append((kind, c))

    def arrived(self, kind, c):
        self.copy(kind, c, True).wait_recv()

    def sent(self, kind):
        for c in (0, 1):
            self.copy(kind, c, False).wait_send()
            self.started.remove((kind, c))

    def finish(self):
        for kind, c in self.started:
            self.copy(kind, c, False).wait_send()
        self.started = []


class Scatter:
    def __init__(self, spot, stage, halves, left, right, crossed, send_sem, recv_sem):
        self.spot, self.stage = spot, stage
        self.halves, self.left, self.right, self.crossed = halves, left, right, crossed
        self.send_sem, self.recv_sem = send_sem, recv_sem
        self.half = halves.shape[1] // 2
        self.started = []

    def copy(self, kind, side, c):
        spot, rows = self.spot, pl.ds(c * self.half, self.half)
        step = 1 if c == 0 else -1
        source, target, lands = {
            0: (self.stage(side, 2), (0, step), self.halves.at[side]),
            1: (self.stage(side, 1), (0, 1), self.left.at[side]),
            2: (self.stage(side, -1), (0, -1), self.right.at[side]),
            3: (self.stage(side, 0), (1, 0), self.crossed),
        }[kind]
        sem = (kind * 2 + side) * 2 + c
        return pltpu.make_async_remote_copy(
            src_ref=source.at[rows],
            dst_ref=lands.at[rows],
            send_sem=self.send_sem.at[sem],
            recv_sem=self.recv_sem.at[sem],
            device_id=spot.device(*target),
            device_id_type=MESH,
        )

    def start(self, kind, side, c):
        self.copy(kind, side, c).start()
        self.started.append((kind, side, c))

    def arrived(self, kind, side, c):
        self.copy(kind, side, c).wait_recv()

    def finish(self):
        for key in self.started:
            self.copy(*key).wait_send()
        self.started = []


class Spread:
    def __init__(self, spot, buf, send_sem, recv_sem):
        self.spot, self.buf, self.send_sem, self.recv_sem = spot, buf, send_sem, recv_sem

    def copy(self, step, landing):
        me = self.spot.index
        other = lax.rem(me + step, GROUP)
        view = self.buf.at[lax.rem(me + GROUP - step, GROUP) if landing else me]
        return pltpu.make_async_remote_copy(
            src_ref=view,
            dst_ref=view,
            send_sem=self.send_sem.at[step - 1],
            recv_sem=self.recv_sem.at[step - 1],
            device_id={self.spot.group: other},
            device_id_type=MESH,
        )

    def start(self):
        for step in range(1, GROUP):
            self.copy(step, False).start()

    def arrived(self):
        for step in range(1, GROUP):
            self.copy(step, True).wait_recv()

    def finish(self):
        for step in range(1, GROUP):
            self.copy(step, False).wait_send()

    def total(self):
        result = self.buf[0]
        for i in range(1, GROUP):
            result = result + self.buf[i]
        return result


def swap_halves(first, second):
    left = lax.broadcasted_iota(jnp.int32, first.shape, 1) < LANES // 2
    return (
        jnp.where(left, first, pltpu.roll(second, LANES // 2, 1)),
        jnp.where(left, pltpu.roll(first, LANES // 2, 1), second),
    )


def tiles(count, body, size=TILE):
    def step(i, carry):
        body(pl.ds(pl.multiple_of(i * size, size), size))
        return carry

    lax.fori_loop(0, count // size, step, 0, unroll=4)


def relay_kernel(
    fwd, kept, cot, weight, bias, gain, shift,
    arrived_out, passed_out, wg_out, bg_out, ng_out,
    xs, ks, cs, w, kown, wg, gst, hhalf, hleft, hright, hcross, ghalf, gleft, gright, gcross,
    vblk, acc, accg, yout, cols, stat, fin, rowt, colg, bsum, pack, land,
    loc_sem, wg_sem,
    c_ss, c_rs, x_ss, x_rs, k_ss, k_rs, h_ss, h_rs, g_ss, g_rs,
    stat_ss, stat_rs, fin_ss, fin_rs, rowt_ss, rowt_rs, colg_ss, colg_rs, a_ss, a_rs,
):
    section = lax.axis_index("section")
    dp, mp = Spot("dp"), Spot("mp")
    rows, width = fwd.shape
    full = width * GROUP
    wide = width // 2

    loads = [
        pltpu.make_async_copy(cot, cs.at[mp.index], loc_sem.at[0]),
        pltpu.make_async_copy(fwd, xs.at[dp.index], loc_sem.at[1]),
        pltpu.make_async_copy(kept, ks.at[dp.index], loc_sem.at[2]),
        pltpu.make_async_copy(kept, kown, loc_sem.at[3]),
        pltpu.make_async_copy(weight, w, loc_sem.at[4]),
    ]
    for i in (1, 2, 0):
        loads[i].start()

    barrier = pltpu.get_barrier_semaphore()
    for spot in (mp, dp):
        for step in range(1, GROUP):
            pl.semaphore_signal(
                barrier, inc=1, device_id={spot.group: lax.rem(spot.index + step, GROUP)}, device_id_type=MESH
            )

    pl.semaphore_signal(barrier, inc=1, device_id={"section": 1 - section}, device_id_type=MESH)

    lane = lax.broadcasted_iota(jnp.int32, (TILE, 128), 1)

    def in_lanes(values):
        result = jnp.zeros((TILE, 128), F32)
        for i, value in enumerate(values):
            result = jnp.where(lane == i, value, result)
        return result

    def row_sums(at):
        x = xs[dp.index, at].astype(F32)
        k = ks[dp.index, at].astype(F32)
        sums = [jnp.sum(v, 1, keepdims=True) for v in (x, x * x, k, k * k)]
        cols[at] = in_lanes(sums)

    loads[1].wait()
    loads[2].wait()
    tiles(rows, row_sums)
    stat[mp.index] = jnp.transpose(cols[...])[0:8]
    loads[0].wait()
    pl.semaphore_wait(barrier, 2 * (GROUP - 1) + 1)

    gc = Gather(mp, cs, c_ss, c_rs, False)
    gx = Gather(dp, xs, x_ss, x_rs, True)
    gk = Gather(dp, ks, k_ss, k_rs, True, 4)
    stats = Spread(mp, stat, stat_ss, stat_rs)
    stats.start()
    for c in (0, 1):
        for gather in (gc, gx):
            gather.start(0, c)
            gather.start(1, c)
            gather.start(2, 1 - c)
    loads[4].start()
    loads[3].start()
    stats.arrived()
    sums = stats.total() / full
    mean_x, mean_k = sums[0:1], sums[2:3]
    inv_x = lax.rsqrt(sums[1:2] - mean_x * mean_x + EPS)
    inv_k = lax.rsqrt(sums[3:4] - mean_k * mean_k + EPS)
    row = lax.broadcasted_iota(jnp.int32, (8, rows), 0)
    fin[dp.index] = jnp.where(row == 0, mean_x, jnp.where(row == 1, inv_x, jnp.where(row == 2, mean_k, inv_k)))
    finished = Spread(dp, fin, fin_ss, fin_rs)
    finished.start()

    def forward(gather):
        gather.arrived(1, 0)
        gather.start(5, 0)
        gather.arrived(2, 1)
        gather.start(5, 1)

    for gather in (gc, gx):
        forward(gather)
    for c in (0, 1):
        for gather in (gc, gx):
            gather.arrived(0, c)
            gather.start(3, c)
            gather.start(4, c)
        if c == 0:
            for d in (0, 1):
                gx.arrived(5, d)
                gx.start(6, d)
    for c in range(3):
        gk.start(1, c)
        gk.start(2, 3 - c)
    gc.arrived(3, 0)
    gc.start(6, 0)
    gc.arrived(4, 1)
    gc.start(6, 1)

    def normalise(buf, slot, out, which):
        cols[:, 0:8] = jnp.transpose(fin[slot])

        def body(at):
            mean = cols[at, which : which + 1]
            inv = cols[at, which + 1 : which + 2]
            hat = (buf[slot, at].astype(F32) - mean) * inv
            out[at] = (hat * gain[...] + shift[...]).astype(BF16)

        tiles(rows, body)

    finished.arrived()
    for steps, kinds, sent in (
        ((0, 0), (), (0, 1, 2)),
        ((0, 1), ((2, 0),), (5,)),
        ((0, -1), ((1, 1),), ()),
        ((1, 0), (), (3, 4)),
        ((1, 1), ((4, 0), (4, 1)), ()),
        ((1, -1), ((3, 0), (3, 1)), ()),
        ((0, 2), (), (6,)),
        ((1, 2), ((6, 0), (6, 1)), ()),
    ):
        for key in kinds:
            gx.arrived(*key)
        for kind in sent:
            gx.sent(kind)
        slot = dp.slot(*steps)
        normalise(xs, slot, xs.at[slot], 0)
    loads[4].wait()
    for kind, c in ((1, 1), (2, 0), (3, 1), (4, 0), (5, 0), (5, 1), (6, 0), (6, 1)):
        gc.arrived(kind, c)
    loads[3].wait()

    def product_h(slot, acc):
        def body(n, carry):
            at = pl.ds(pl.multiple_of(n * wide, MXU), wide)
            acc[:, at] = jnp.dot(xs[slot], w[:, at], preferred_element_type=F32)
            return carry

        lax.fori_loop(0, width // wide, body, 0)

    def product_g(slot, acc):
        def body(n, carry):
            at = pl.ds(pl.multiple_of(n * wide, MXU), wide)
            acc[:, at] = lax.dot_general(
                cs[slot], w[at, :], (((1,), (1,)), ((), ())), preferred_element_type=F32
            )
            return carry

        lax.fori_loop(0, width // wide, body, 0)

    def product_w(pair_step, ring_step, fresh=False):
        slot = dp.slot(pair_step, ring_step)
        normalise(ks, slot, vblk, 2)

        def body(n, carry):
            at = pl.ds(pl.multiple_of(n * wide, MXU), wide)
            term = lax.dot_general(
                vblk[:, at], cs[slot], (((0,), (0,)), ((), ())), preferred_element_type=F32
            )
            wg[at, :] = term if fresh else wg[at, :] + term
            return carry

        lax.fori_loop(0, width // wide, body, 0)

    half = rows // 2

    def emit(stage, start, terms, acc):
        def body(i, carry):
            at = pl.ds(pl.multiple_of(start + i * TILE, TILE), TILE)
            value = acc[at]
            for term in terms:
                value = value + term[at].astype(F32)
            stage[at] = value.astype(BF16)
            return carry

        lax.fori_loop(0, half // TILE, body, 0, unroll=4)

    def stage_g(side, ring_step):
        place = {2: 0, 1: 1, -1: 2, 0: 3}[ring_step] * 2 + side
        return gst.at[place]

    def stage_h(side, ring_step):
        return xs.at[mp.slot(1 - side, ring_step)]

    rg = Scatter(dp, stage_g, ghalf, gleft, gright, gcross, g_ss, g_rs)
    rh = Scatter(mp, stage_h, hhalf, hleft, hright, hcross, h_ss, h_rs)
    work_g, work_h = (rg, product_g), (rh, product_h)

    def far(scatter, product, side):
        product(scatter.spot.slot(1 - side, 2), acc)
        for c in (0, 1):
            emit(scatter.stage(side, 2), c * half, [], acc)
            scatter.start(0, side, c)

    def near(scatter, product, side):
        product(scatter.spot.slot(1 - side, 1), acc)
        scatter.arrived(0, side, 0)
        for c in (0, 1):
            emit(scatter.stage(side, 1), c * half, [] if c else [scatter.halves.at[side]], acc)
            scatter.start(1, side, c)
        product(scatter.spot.slot(1 - side, -1), acc)
        for c in (0, 1):
            if c:
                scatter.arrived(0, side, 1)
            emit(scatter.stage(side, -1), c * half, [scatter.halves.at[side]] if c else [], acc)
            scatter.start(2, side, c)

    def cross(scatter, c, acc):
        scatter.arrived(1, 0, c)
        scatter.arrived(2, 0, c)
        emit(scatter.stage(0, 0), c * half, [scatter.left.at[0], scatter.right.at[0]], acc)
        scatter.start(3, 0, c)

    far(*work_g, 0)
    far(*work_h, 0)
    for c in range(4):
        gk.start(0, c)
    for kind, c in ((1, 0), (2, 3)):
        gk.arrived(kind, c)
        gk.start(kind + 6, c)
    near(*work_g, 0)
    near(*work_h, 0)
    far(*work_g, 1)
    far(*work_h, 1)
    gk.start(5, 0)
    gk.start(5, 3)
    gk.arrived(1, 1)
    gk.start(5, 1)
    gk.arrived(2, 2)
    gk.start(5, 2)
    product_g(dp.slot(1, 0), accg)
    cross(rg, 0, accg)
    near(*work_g, 1)
    near(*work_h, 1)
    cross(rg, 1, accg)
    product_h(mp.slot(1, 0), accg)
    cross(rh, 0, accg)
    cross(rh, 1, accg)
    gk.start(1, 3)
    gk.start(2, 0)
    for c in range(4):
        gk.arrived(0, c)
        if c != 0:
            gk.start(3, c)
        if c != 3:
            gk.start(4, c)
    for c in range(4):
        gk.arrived(5, c)
        gk.start(6, c)

    bsum[...] = jnp.zeros_like(bsum)

    def add_block(slot, carry):
        def add(at):
            c = cs[slot, at].astype(F32)
            bsum[...] += c[0:8] + c[8:16]

        tiles(rows, add)
        return carry

    lax.fori_loop(0, GROUP, add_block, 0)
    product_w(0, 0, True)
    product_w(1, 0)
    product_w(0, 2)

    def whole(scatter, acc, finish):
        for c in (0, 1):
            for kind, side in ((1, 1), (2, 1), (3, 0)):
                scatter.arrived(kind, side, c)

        def body(at):
            value = acc[at]
            for term in (scatter.left.at[1], scatter.right.at[1], scatter.crossed):
                value = value + term[at].astype(F32)
            finish(at, value)

        tiles(rows, body)

    def hat_kept(at):
        return (kown[at].astype(F32) - cols[at, 2:3]) * cols[at, 3:4]

    def finish_g(at, value):
        hat = hat_kept(at)
        colg[dp.index, 0:1] += jnp.sum(value * hat, 0, keepdims=True)
        colg[dp.index, 1:2] += jnp.sum(value, 0, keepdims=True)
        accg[at] = value
        scaled = value * gain[...]
        terms = [jnp.sum(v, 1, keepdims=True) for v in (scaled, scaled * hat)]
        lanes = in_lanes(terms)
        cols[at, 8:16] = lanes[:, 0:8]

    product_g(dp.slot(0, 0), accg)
    product_h(mp.slot(0, 0), acc)
    cols[:, 0:8] = jnp.transpose(fin[dp.index])
    colg[dp.index] = jnp.zeros(colg.shape[1:], F32)
    whole(rg, accg, finish_g)
    terms = Spread(mp, rowt, rowt_ss, rowt_rs)
    rowt[mp.index] = jnp.transpose(cols[...])[8:16]
    terms.start()
    column = Spread(dp, colg, colg_ss, colg_rs)
    column.start()

    piece_rows = rows // GROUP
    first = section == 0
    row_at = jnp.where(first, mp.index, dp.index)
    col_at = jnp.where(first, dp.index, mp.index)

    def piece(i):
        j = lax.rem(i + dp.index * GROUP + mp.index, GROUP * GROUP)
        b, f = lax.div(j, GROUP), lax.rem(j, GROUP)
        return pltpu.make_async_remote_copy(
            src_ref=pack.at[b, f],
            dst_ref=land.at[row_at, col_at],
            send_sem=a_ss,
            recv_sem=a_rs,
            device_id={"section": 1 - section, "dp": jnp.where(first, b, f), "mp": jnp.where(first, f, b)},
            device_id_type=MESH,
        )

    def send_piece(i, carry):
        piece(i).start()
        return carry

    odd = lax.rem(col_at, 2) == 1
    low = lax.broadcasted_iota(jnp.int32, (piece_rows, LANES), 1) < LANES // 2

    def halves(value):
        return value[: piece_rows // 2], value[piece_rows // 2 :]

    def relay(values):
        def packing(b, carry):
            at = pl.ds(pl.multiple_of(b * piece_rows, piece_rows), piece_rows)
            sent = values[at]
            for k in range(GROUP // 2):
                left, shared, right = (sent[:, (3 * k + i) * LANES : (3 * k + i + 1) * LANES] for i in range(3))
                turned = [pltpu.roll(v, LANES // 2, 1) for v in (left, shared, right)]
                early = jnp.where(odd, jnp.where(low, turned[0], turned[1]), left)
                later = jnp.where(odd, right, jnp.where(low, turned[1], turned[2]))
                early_half = swap_halves(*halves(jnp.where(odd, left, shared)))[0]
                later_half = swap_halves(*halves(jnp.where(odd, shared, right)))[1]
                pack[b, 2 * k, 0:piece_rows] = early.astype(BF16)
                pack[b, 2 * k + 1, 0:piece_rows] = later.astype(BF16)
                pack[b, 2 * k, piece_rows:] = early_half.astype(BF16)
                pack[b, 2 * k + 1, piece_rows:] = later_half.astype(BF16)
            return carry

        lax.fori_loop(0, GROUP, packing, 0)
        lax.fori_loop(0, GROUP * GROUP, send_piece, 0)

    def finish_h(at, value):
        acc[at] = value + bias[...]

    whole(rh, acc, finish_h)

    @pl.when(first)
    def _():
        relay(acc)

    terms.arrived()
    cols[:, 8:16] = jnp.transpose(terms.total() / full)

    def input_grad(at):
        hat = hat_kept(at)
        scaled = accg[at] * gain[...]
        accg[at] = cols[at, 3:4] * (scaled - cols[at, 8:9] - hat * cols[at, 9:10])

    tiles(rows, input_grad)

    @pl.when(section == 1)
    def _():
        relay(accg)

    def keeping(at):
        yout[at] = jnp.where(first, accg[at], acc[at]).astype(BF16)

    tiles(rows, keeping)
    keep = pltpu.make_async_copy(yout, passed_out, loc_sem.at[0])
    keep.start()

    for steps, kinds in (
        ((0, 1), ((2, 1), (2, 0))),
        ((0, -1), ((1, 2), (1, 3))),
        ((1, 1), ((4, 0), (4, 1), (4, 2), (8, 3))),
        ((1, -1), ((3, 1), (3, 2), (3, 3), (7, 0))),
    ):
        for key in kinds:
            gk.arrived(*key)
        product_w(*steps)
    every_piece = pltpu.make_async_remote_copy(
        src_ref=pack,
        dst_ref=land,
        send_sem=a_ss,
        recv_sem=a_rs,
        device_id={"section": 1 - section},
        device_id_type=MESH,
    )
    every_piece.wait_recv()
    out = pltpu.make_async_copy(land, arrived_out, loc_sem.at[1])
    out.start()
    for c in range(4):
        gk.arrived(6, c)
    rh.finish()
    slot = dp.slot(1, 2)
    normalise(ks, slot, vblk, 2)

    def store(n):
        at = pl.ds(pl.multiple_of(n * rows, rows), rows)
        return pltpu.make_async_copy(xs.at[n], wg_out.at[at], wg_sem.at[n])

    def last(n, carry):
        at = pl.ds(pl.multiple_of(n * rows, rows), rows)
        term = lax.dot_general(vblk[:, at], cs[slot], (((0,), (0,)), ((), ())), preferred_element_type=F32)
        xs[n] = (wg[at, :] + term).astype(BF16)
        store(n).start()
        return carry

    lax.fori_loop(0, width // rows, last, 0)

    bg_out[...] = jnp.sum(bsum[...], 0, keepdims=True)
    column.arrived()
    ng_out[...] = column.total()

    every_piece.wait_send()
    for transfer in (gc, gk, rg, rh, stats, finished, column, terms):
        transfer.finish()
    keep.wait()
    for n in range(width // rows):
        store(n).wait()
    out.wait()


def finish_kernel(
    arrived, passed, grad, bias_grad, norm_grads, next_out, passed_out, wg_out, bg_out, ng_out
):
    wg_out[...] = grad[...].astype(F32)

    @pl.when(pl.program_id(0) == 0)
    def _():
        piece_rows = next_out.shape[0] // GROUP

        def body(a, carry):
            at = pl.ds(pl.multiple_of(a * piece_rows, piece_rows), piece_rows)
            for k in range(GROUP // 2):
                even, odd = arrived[a, 2 * k], arrived[a, 2 * k + 1]
                shared = swap_halves(even[piece_rows:].astype(F32), odd[piece_rows:].astype(F32))
                columns = (even[:piece_rows], jnp.concatenate(shared, axis=0).astype(BF16), odd[:piece_rows])
                for i, column in enumerate(columns):
                    next_out[at, (3 * k + i) * LANES : (3 * k + i + 1) * LANES] = column
            return carry

        lax.fori_loop(0, GROUP, body, 0)
        passed_out[...] = passed[...]
        bg_out[...] = bias_grad[...]
        ng_out[...] = norm_grads[...]


def shards(fwd_in, kept_in, cotangent, weight, bias, norm_gain, norm_shift):
    section_index = lax.axis_index("section")
    rows, cols = fwd_in.shape[3:]
    piece = (GROUP, GROUP, rows // GROUP * 3 // 2, LANES)
    any_spec = pl.BlockSpec(memory_space=pl.ANY)
    vmem_spec = pl.BlockSpec(memory_space=pltpu.VMEM)
    dma = pltpu.SemaphoreType.DMA
    shard = pltpu.VMEM((rows, cols), BF16)
    gathered = pltpu.VMEM((GROUP, rows, cols), BF16)
    two = pltpu.VMEM((2, rows, cols), BF16)
    arrived, passed, grad, bias_grad, norm_grads = pl.pallas_call(
        relay_kernel,
        name="relay",
        out_shape=(
            jax.ShapeDtypeStruct(piece, BF16),
            jax.ShapeDtypeStruct((rows, cols), BF16),
            jax.ShapeDtypeStruct((cols, cols), BF16),
            jax.ShapeDtypeStruct((1, cols), F32),
            jax.ShapeDtypeStruct((2, cols), F32),
        ),
        in_specs=[any_spec] * 4 + [vmem_spec] * 3,
        out_specs=(any_spec,) * 3 + (vmem_spec,) * 2,
        scratch_shapes=[
            gathered, gathered, gathered, pltpu.VMEM((cols, cols), BF16), shard, pltpu.VMEM((cols, cols), F32),
            pltpu.VMEM((7, rows, cols), BF16),
            two, two, two, shard, two, two, two, shard,
            shard, pltpu.VMEM((rows, cols), F32), pltpu.VMEM((rows, cols), F32), shard, pltpu.VMEM((rows, 128), F32),
            pltpu.VMEM((GROUP, 8, rows), F32), pltpu.VMEM((GROUP, 8, rows), F32), pltpu.VMEM((GROUP, 8, rows), F32),
            pltpu.VMEM((GROUP, 2, cols), F32), pltpu.VMEM((8, cols), F32),
            pltpu.VMEM(piece, BF16), pltpu.VMEM(piece, BF16),
            dma((5,)), dma((cols // rows,)),
            dma((7, 2)), dma((7, 2)), dma((7, 2)), dma((7, 2)), dma((9, 4)), dma((9, 4)),
            dma((16,)), dma((16,)), dma((16,)), dma((16,)),
            dma((7,)), dma((7,)), dma((7,)), dma((7,)), dma((7,)), dma((7,)), dma((7,)), dma((7,)),
            dma, dma,
        ],
        compiler_params=pltpu.CompilerParams(
            collective_id=0, has_side_effects=True, vmem_limit_bytes=60 * 2**20
        ),
    )(
        fwd_in.reshape(rows, cols),
        kept_in.reshape(rows, cols),
        cotangent.reshape(rows, cols),
        weight.reshape(cols, cols),
        bias.reshape(1, cols),
        norm_gain.reshape(1, cols),
        norm_shift.reshape(1, cols),
    )
    fixed = lambda *shape: pl.BlockSpec(shape, lambda i: (0,) * len(shape))
    tile = pl.BlockSpec((MXU, cols), lambda i: (i, 0))
    next_in, passed, weight_grad, bias_grad, norm_grads = pl.pallas_call(
        finish_kernel,
        name="finish",
        grid=(cols // MXU,),
        out_shape=(
            jax.ShapeDtypeStruct((rows, cols), BF16),
            jax.ShapeDtypeStruct((rows, cols), BF16),
            jax.ShapeDtypeStruct((cols, cols), F32),
            jax.ShapeDtypeStruct((1, cols), F32),
            jax.ShapeDtypeStruct((2, cols), F32),
        ),
        in_specs=[
            fixed(*piece),
            fixed(rows, cols),
            tile,
            fixed(1, cols),
            fixed(2, cols),
        ],
        out_specs=(fixed(rows, cols), fixed(rows, cols), tile, fixed(1, cols), fixed(2, cols)),
        compiler_params=pltpu.CompilerParams(vmem_limit_bytes=60 * 2**20),
    )(arrived, passed, grad, bias_grad, norm_grads)
    return (
        next_in.reshape(fwd_in.shape),
        passed.reshape(fwd_in.shape),
        weight_grad.reshape(1, cols, cols),
        bias_grad,
        norm_grads.reshape(1, 2, cols),
    )


def solution(mesh):
    placed = (
        P("section", "dp", "mp", None, None),
        P("section", "dp", "mp", None, None),
        P("section", "dp", "mp", None, None),
        P("section", "mp", "dp"),
        P("section", "dp"),
        P("section", "mp"),
        P("section", "mp"),
    )
    return jax.shard_map(
        shards,
        mesh=mesh,
        in_specs=placed,
        out_specs=(
            P("section", "dp", "mp", None, None),
            P("section", "dp", "mp", None, None),
            P("section", "mp", "dp"),
            P("section", "dp"),
            P("section", None, "mp"),
        ),
        check_vma=False,
    )
```

```python
import jax
import jax.numpy as jnp
from jax import lax
from jax.experimental import pallas as pl
from jax.experimental.pallas import tpu as pltpu
from jax.sharding import PartitionSpec as P

EPS = 1e-05
RING = 4
PAIR = 2
GROUP = RING * PAIR
TILE = 16
MXU = 256
LANES = 128
F32 = jnp.float32
BF16 = jnp.bfloat16
MESH = pl.DeviceIdType.MESH


class Spot:
    def __init__(self, group):
        self.group = group
        self.index = lax.axis_index(group)
        self.pair = lax.div(self.index, RING)
        self.ring = lax.rem(self.index, RING)

    def slot(self, pair_step, ring_step):
        pair = lax.rem(self.pair + pair_step, PAIR)
        return pair * RING + lax.rem(self.ring + ring_step + RING, RING)

    def device(self, pair_step, ring_step):
        return {self.group: self.slot(pair_step, ring_step)}


class Gather:
    def __init__(self, spot, buf, send_sem, recv_sem, far_by_pair, parts=2):
        self.spot, self.buf, self.far_by_pair, self.parts = spot, buf, far_by_pair, parts
        self.send_sem, self.recv_sem = send_sem, recv_sem
        self.part = buf.shape[1] // parts
        self.started = []

    def route(self, kind, c):
        step = 1 if c < self.parts // 2 else -1
        return {
            0: ((0, 0), (1, 0), (1, 0)),
            1: ((0, 0), (0, 1), (0, -1)),
            2: ((0, 0), (0, -1), (0, 1)),
            3: ((1, 0), (0, 1), (1, -1)),
            4: ((1, 0), (0, -1), (1, 1)),
            5: ((0, -step), (0, step), (0, 2)),
            7: ((0, -1), (1, 0), (1, -1)),
            9: ((1, -step), (0, step), (1, 2)),
            8: ((0, 1), (1, 0), (1, 1)),
            6: ((0, 2), (1, 0), (1, 2)) if self.far_by_pair else ((1, -step), (0, step), (1, 2)),
        }[kind]

    def copy(self, kind, c, landing):
        source, target, lands = self.route(kind, c)
        here = self.spot.slot(*(lands if landing else source))
        view = self.buf.at[here, pl.ds(c * self.part, self.part)]
        return pltpu.make_async_remote_copy(
            src_ref=view,
            dst_ref=view,
            send_sem=self.send_sem.at[kind, c],
            recv_sem=self.recv_sem.at[kind, c],
            device_id=self.spot.device(*target),
            device_id_type=MESH,
        )

    def start(self, kind, c):
        self.copy(kind, c, False).start()
        self.started.append((kind, c))

    def arrived(self, kind, c):
        self.copy(kind, c, True).wait_recv()

    def sent(self, kind):
        for c in (0, 1):
            self.copy(kind, c, False).wait_send()
            self.started.remove((kind, c))

    def finish(self):
        for kind, c in self.started:
            self.copy(kind, c, False).wait_send()
        self.started = []


class Scatter:
    def __init__(self, spot, stage, halves, left, right, crossed, send_sem, recv_sem):
        self.spot, self.stage = spot, stage
        self.halves, self.left, self.right, self.crossed = halves, left, right, crossed
        self.send_sem, self.recv_sem = send_sem, recv_sem
        self.half = halves.shape[1] // 2
        self.started = []

    def copy(self, kind, side, c):
        spot, rows = self.spot, pl.ds(c * self.half, self.half)
        step = 1 if c == 0 else -1
        source, target, lands = {
            0: (self.stage(side, 2), (0, step), self.halves.at[side]),
            1: (self.stage(side, 1), (0, 1), self.left.at[side]),
            2: (self.stage(side, -1), (0, -1), self.right.at[side]),
            3: (self.stage(side, 0), (1, 0), self.crossed),
        }[kind]
        sem = (kind * 2 + side) * 2 + c
        return pltpu.make_async_remote_copy(
            src_ref=source.at[rows],
            dst_ref=lands.at[rows],
            send_sem=self.send_sem.at[sem],
            recv_sem=self.recv_sem.at[sem],
            device_id=spot.device(*target),
            device_id_type=MESH,
        )

    def start(self, kind, side, c):
        self.copy(kind, side, c).start()
        self.started.append((kind, side, c))

    def arrived(self, kind, side, c):
        self.copy(kind, side, c).wait_recv()

    def finish(self):
        for key in self.started:
            self.copy(*key).wait_send()
        self.started = []


class Spread:
    def __init__(self, spot, buf, send_sem, recv_sem):
        self.spot, self.buf, self.send_sem, self.recv_sem = spot, buf, send_sem, recv_sem

    def copy(self, step, landing):
        me = self.spot.index
        other = lax.rem(me + step, GROUP)
        view = self.buf.at[lax.rem(me + GROUP - step, GROUP) if landing else me]
        return pltpu.make_async_remote_copy(
            src_ref=view,
            dst_ref=view,
            send_sem=self.send_sem.at[step - 1],
            recv_sem=self.recv_sem.at[step - 1],
            device_id={self.spot.group: other},
            device_id_type=MESH,
        )

    def start(self):
        for step in range(1, GROUP):
            self.copy(step, False).start()

    def arrived(self):
        for step in range(1, GROUP):
            self.copy(step, True).wait_recv()

    def finish(self):
        for step in range(1, GROUP):
            self.copy(step, False).wait_send()

    def total(self):
        result = self.buf[0]
        for i in range(1, GROUP):
            result = result + self.buf[i]
        return result


def swap_halves(first, second):
    left = lax.broadcasted_iota(jnp.int32, first.shape, 1) < LANES // 2
    return (
        jnp.where(left, first, pltpu.roll(second, LANES // 2, 1)),
        jnp.where(left, pltpu.roll(first, LANES // 2, 1), second),
    )


def tiles(count, body, size=TILE):
    def step(i, carry):
        body(pl.ds(pl.multiple_of(i * size, size), size))
        return carry

    lax.fori_loop(0, count // size, step, 0, unroll=4)


def relay_kernel(
    fwd, kept, cot, weight, bias, gain, shift,
    arrived_out, passed_out, wg_out, bg_out, ng_out,
    xs, ks, cs, w, kown, wg, gst, hhalf, hleft, hright, hcross, ghalf, gleft, gright, gcross,
    vblk, acc, accg, yout, cols, stat, fin, rowt, colg, bsum, pack, land,
    loc_sem, wg_sem,
    c_ss, c_rs, x_ss, x_rs, k_ss, k_rs, h_ss, h_rs, g_ss, g_rs,
    stat_ss, stat_rs, fin_ss, fin_rs, rowt_ss, rowt_rs, colg_ss, colg_rs, a_ss, a_rs,
):
    section = lax.axis_index("section")
    dp, mp = Spot("dp"), Spot("mp")
    rows, width = fwd.shape
    full = width * GROUP
    wide = width // 2

    loads = [
        pltpu.make_async_copy(cot, cs.at[mp.index], loc_sem.at[0]),
        pltpu.make_async_copy(fwd, xs.at[dp.index], loc_sem.at[1]),
        pltpu.make_async_copy(kept, ks.at[dp.index], loc_sem.at[2]),
        pltpu.make_async_copy(kept, kown, loc_sem.at[3]),
        pltpu.make_async_copy(weight, w, loc_sem.at[4]),
    ]
    for i in (1, 2, 0):
        loads[i].start()

    barrier = pltpu.get_barrier_semaphore()
    for spot in (mp, dp):
        for step in range(1, GROUP):
            pl.semaphore_signal(
                barrier, inc=1, device_id={spot.group: lax.rem(spot.index + step, GROUP)}, device_id_type=MESH
            )

    pl.semaphore_signal(barrier, inc=1, device_id={"section": 1 - section}, device_id_type=MESH)

    lane = lax.broadcasted_iota(jnp.int32, (TILE, 128), 1)

    def in_lanes(values):
        result = jnp.zeros((TILE, 128), F32)
        for i, value in enumerate(values):
            result = jnp.where(lane == i, value, result)
        return result

    def row_sums(at):
        x = xs[dp.index, at].astype(F32)
        k = ks[dp.index, at].astype(F32)
        sums = [jnp.sum(v, 1, keepdims=True) for v in (x, x * x, k, k * k)]
        cols[at] = in_lanes(sums)

    loads[1].wait()
    loads[2].wait()
    tiles(rows, row_sums)
    stat[mp.index] = jnp.transpose(cols[...])[0:8]
    loads[0].wait()
    pl.semaphore_wait(barrier, 2 * (GROUP - 1) + 1)

    gc = Gather(mp, cs, c_ss, c_rs, False)
    gx = Gather(dp, xs, x_ss, x_rs, True)
    gk = Gather(dp, ks, k_ss, k_rs, True, 4)
    stats = Spread(mp, stat, stat_ss, stat_rs)
    stats.start()
    for c in (0, 1):
        for gather in (gc, gx):
            gather.start(0, c)
            gather.start(1, c)
            gather.start(2, 1 - c)
    loads[4].start()
    loads[3].start()
    stats.arrived()
    sums = stats.total() / full
    mean_x, mean_k = sums[0:1], sums[2:3]
    inv_x = lax.rsqrt(sums[1:2] - mean_x * mean_x + EPS)
    inv_k = lax.rsqrt(sums[3:4] - mean_k * mean_k + EPS)
    row = lax.broadcasted_iota(jnp.int32, (8, rows), 0)
    fin[dp.index] = jnp.where(row == 0, mean_x, jnp.where(row == 1, inv_x, jnp.where(row == 2, mean_k, inv_k)))
    finished = Spread(dp, fin, fin_ss, fin_rs)
    finished.start()

    def forward(gather):
        gather.arrived(1, 0)
        gather.start(5, 0)
        gather.arrived(2, 1)
        gather.start(5, 1)

    for gather in (gc, gx):
        forward(gather)
    for c in (0, 1):
        for gather in (gc, gx):
            gather.arrived(0, c)
            gather.start(3, c)
            gather.start(4, c)
        if c == 0:
            for d in (0, 1):
                gx.arrived(5, d)
                gx.start(6, d)
    for c in range(3):
        gk.start(1, c)
        gk.start(2, 3 - c)
    for c in range(4):
        gk.start(0, c)
    gc.arrived(3, 0)
    gc.start(6, 0)
    gc.arrived(4, 1)
    gc.start(6, 1)

    def normalise(buf, slot, out, which):
        cols[:, 0:8] = jnp.transpose(fin[slot])

        def body(at):
            mean = cols[at, which : which + 1]
            inv = cols[at, which + 1 : which + 2]
            hat = (buf[slot, at].astype(F32) - mean) * inv
            out[at] = (hat * gain[...] + shift[...]).astype(BF16)

        tiles(rows, body)

    finished.arrived()
    for steps, kinds, sent in (
        ((0, 0), (), (0, 1, 2)),
        ((0, 1), ((2, 0),), (5,)),
        ((0, -1), ((1, 1),), ()),
        ((1, 0), (), (3, 4)),
        ((1, 1), ((4, 0), (4, 1)), ()),
        ((1, -1), ((3, 0), (3, 1)), ()),
        ((0, 2), (), (6,)),
        ((1, 2), ((6, 0), (6, 1)), ()),
    ):
        for key in kinds:
            gx.arrived(*key)
        for kind in sent:
            gx.sent(kind)
        slot = dp.slot(*steps)
        normalise(xs, slot, xs.at[slot], 0)
    loads[4].wait()
    for kind, c in ((1, 1), (2, 0), (3, 1), (4, 0), (5, 0), (5, 1), (6, 0), (6, 1)):
        gc.arrived(kind, c)
    loads[3].wait()

    def product_h(slot, acc):
        def body(n, carry):
            at = pl.ds(pl.multiple_of(n * wide, MXU), wide)
            acc[:, at] = jnp.dot(xs[slot], w[:, at], preferred_element_type=F32)
            return carry

        lax.fori_loop(0, width // wide, body, 0)

    def product_g(slot, acc):
        def body(n, carry):
            at = pl.ds(pl.multiple_of(n * wide, MXU), wide)
            acc[:, at] = lax.dot_general(
                cs[slot], w[at, :], (((1,), (1,)), ((), ())), preferred_element_type=F32
            )
            return carry

        lax.fori_loop(0, width // wide, body, 0)

    def product_w(pair_step, ring_step, fresh=False):
        slot = dp.slot(pair_step, ring_step)
        normalise(ks, slot, vblk, 2)

        def body(n, carry):
            at = pl.ds(pl.multiple_of(n * wide, MXU), wide)
            term = lax.dot_general(
                vblk[:, at], cs[slot], (((0,), (0,)), ((), ())), preferred_element_type=F32
            )
            wg[at, :] = term if fresh else wg[at, :] + term
            return carry

        lax.fori_loop(0, width // wide, body, 0)

    half = rows // 2

    def emit(stage, start, terms, acc):
        def body(i, carry):
            at = pl.ds(pl.multiple_of(start + i * TILE, TILE), TILE)
            value = acc[at]
            for term in terms:
                value = value + term[at].astype(F32)
            stage[at] = value.astype(BF16)
            return carry

        lax.fori_loop(0, half // TILE, body, 0, unroll=4)

    def stage_g(side, ring_step):
        place = {2: 0, 1: 1, -1: 2, 0: 3}[ring_step] * 2 + side
        return gst.at[place]

    def stage_h(side, ring_step):
        return xs.at[mp.slot(1 - side, ring_step)]

    rg = Scatter(dp, stage_g, ghalf, gleft, gright, gcross, g_ss, g_rs)
    rh = Scatter(mp, stage_h, hhalf, hleft, hright, hcross, h_ss, h_rs)
    work_g, work_h = (rg, product_g), (rh, product_h)

    def far(scatter, product, side):
        product(scatter.spot.slot(1 - side, 2), acc)
        for c in (0, 1):
            emit(scatter.stage(side, 2), c * half, [], acc)
            scatter.start(0, side, c)

    def near(scatter, product, side):
        product(scatter.spot.slot(1 - side, 1), acc)
        scatter.arrived(0, side, 0)
        for c in (0, 1):
            emit(scatter.stage(side, 1), c * half, [] if c else [scatter.halves.at[side]], acc)
            scatter.start(1, side, c)
        product(scatter.spot.slot(1 - side, -1), acc)
        for c in (0, 1):
            if c:
                scatter.arrived(0, side, 1)
            emit(scatter.stage(side, -1), c * half, [scatter.halves.at[side]] if c else [], acc)
            scatter.start(2, side, c)

    def cross(scatter, c, acc):
        scatter.arrived(1, 0, c)
        scatter.arrived(2, 0, c)
        emit(scatter.stage(0, 0), c * half, [scatter.left.at[0], scatter.right.at[0]], acc)
        scatter.start(3, 0, c)

    far(*work_g, 0)
    far(*work_h, 0)
    for kind, c in ((1, 0), (2, 3)):
        gk.arrived(kind, c)
        gk.start(kind + 6, c)
    near(*work_g, 0)
    near(*work_h, 0)
    far(*work_g, 1)
    far(*work_h, 1)
    gk.start(1, 3)
    gk.start(2, 0)
    gk.start(5, 0)
    gk.start(5, 3)
    gk.arrived(1, 1)
    gk.start(5, 1)
    gk.arrived(2, 2)
    gk.start(5, 2)
    product_g(dp.slot(1, 0), accg)
    cross(rg, 0, accg)
    near(*work_g, 1)
    near(*work_h, 1)
    cross(rg, 1, accg)
    product_h(mp.slot(1, 0), accg)
    cross(rh, 0, accg)
    cross(rh, 1, accg)
    for c in range(4):
        gk.arrived(0, c)
        if c != 0:
            gk.start(3, c)
        if c != 3:
            gk.start(4, c)
    for c in range(4):
        gk.arrived(5, c)
        if c in (1, 2):
            gk.start(6, c)
    for kind, c in ((7, 0), (8, 3)):
        gk.arrived(kind, c)
        gk.start(9, c)

    bsum[...] = jnp.zeros_like(bsum)

    def add_block(slot, carry):
        def add(at):
            c = cs[slot, at].astype(F32)
            bsum[...] += c[0:8] + c[8:16]

        tiles(rows, add)
        return carry

    lax.fori_loop(0, GROUP, add_block, 0)
    product_w(0, 0, True)
    product_w(1, 0)
    product_w(0, 2)
    for kind, c in ((2, 1), (2, 0), (1, 2), (1, 3)):
        gk.arrived(kind, c)
    product_w(0, 1)
    product_w(0, -1)

    def whole(scatter, acc, finish):
        for c in (0, 1):
            for kind, side in ((1, 1), (2, 1), (3, 0)):
                scatter.arrived(kind, side, c)

        def body(at):
            value = acc[at]
            for term in (scatter.left.at[1], scatter.right.at[1], scatter.crossed):
                value = value + term[at].astype(F32)
            finish(at, value)

        tiles(rows, body)

    def hat_kept(at):
        return (kown[at].astype(F32) - cols[at, 2:3]) * cols[at, 3:4]

    def finish_g(at, value):
        hat = hat_kept(at)
        colg[dp.index, 0:1] += jnp.sum(value * hat, 0, keepdims=True)
        colg[dp.index, 1:2] += jnp.sum(value, 0, keepdims=True)
        accg[at] = value
        scaled = value * gain[...]
        terms = [jnp.sum(v, 1, keepdims=True) for v in (scaled, scaled * hat)]
        lanes = in_lanes(terms)
        cols[at, 8:16] = lanes[:, 0:8]

    product_g(dp.slot(0, 0), accg)
    product_h(mp.slot(0, 0), acc)
    cols[:, 0:8] = jnp.transpose(fin[dp.index])
    colg[dp.index] = jnp.zeros(colg.shape[1:], F32)
    whole(rg, accg, finish_g)
    terms = Spread(mp, rowt, rowt_ss, rowt_rs)
    rowt[mp.index] = jnp.transpose(cols[...])[8:16]
    terms.start()
    column = Spread(dp, colg, colg_ss, colg_rs)
    column.start()

    piece_rows = rows // GROUP
    first = section == 0
    row_at = jnp.where(first, mp.index, dp.index)
    col_at = jnp.where(first, dp.index, mp.index)

    def piece(i):
        j = lax.rem(i + dp.index * GROUP + mp.index, GROUP * GROUP)
        b, f = lax.div(j, GROUP), lax.rem(j, GROUP)
        return pltpu.make_async_remote_copy(
            src_ref=pack.at[b, f],
            dst_ref=land.at[row_at, col_at],
            send_sem=a_ss,
            recv_sem=a_rs,
            device_id={"section": 1 - section, "dp": jnp.where(first, b, f), "mp": jnp.where(first, f, b)},
            device_id_type=MESH,
        )

    def send_piece(i, carry):
        piece(i).start()
        return carry

    odd = lax.rem(col_at, 2) == 1
    low = lax.broadcasted_iota(jnp.int32, (piece_rows, LANES), 1) < LANES // 2

    def halves(value):
        return value[: piece_rows // 2], value[piece_rows // 2 :]

    def relay(values):
        def packing(b, carry):
            at = pl.ds(pl.multiple_of(b * piece_rows, piece_rows), piece_rows)
            sent = values[at]
            for k in range(GROUP // 2):
                left, shared, right = (sent[:, (3 * k + i) * LANES : (3 * k + i + 1) * LANES] for i in range(3))
                turned = [pltpu.roll(v, LANES // 2, 1) for v in (left, shared, right)]
                early = jnp.where(odd, jnp.where(low, turned[0], turned[1]), left)
                later = jnp.where(odd, right, jnp.where(low, turned[1], turned[2]))
                early_half = swap_halves(*halves(jnp.where(odd, left, shared)))[0]
                later_half = swap_halves(*halves(jnp.where(odd, shared, right)))[1]
                pack[b, 2 * k, 0:piece_rows] = early.astype(BF16)
                pack[b, 2 * k + 1, 0:piece_rows] = later.astype(BF16)
                pack[b, 2 * k, piece_rows:] = early_half.astype(BF16)
                pack[b, 2 * k + 1, piece_rows:] = later_half.astype(BF16)
            return carry

        lax.fori_loop(0, GROUP, packing, 0)
        lax.fori_loop(0, GROUP * GROUP, send_piece, 0)

    def finish_h(at, value):
        acc[at] = value + bias[...]

    whole(rh, acc, finish_h)

    @pl.when(first)
    def _():
        relay(acc)

    terms.arrived()
    cols[:, 8:16] = jnp.transpose(terms.total() / full)

    def input_grad(at):
        hat = hat_kept(at)
        scaled = accg[at] * gain[...]
        accg[at] = cols[at, 3:4] * (scaled - cols[at, 8:9] - hat * cols[at, 9:10])

    tiles(rows, input_grad)

    @pl.when(section == 1)
    def _():
        relay(accg)

    def keeping(at):
        yout[at] = jnp.where(first, accg[at], acc[at]).astype(BF16)

    tiles(rows, keeping)
    keep = pltpu.make_async_copy(yout, passed_out, loc_sem.at[0])
    keep.start()

    for steps, kinds in (
        ((1, 1), ((4, 0), (4, 1), (4, 2))),
        ((1, -1), ((3, 1), (3, 2), (3, 3))),
    ):
        for key in kinds:
            gk.arrived(*key)
        product_w(*steps)
    every_piece = pltpu.make_async_remote_copy(
        src_ref=pack,
        dst_ref=land,
        send_sem=a_ss,
        recv_sem=a_rs,
        device_id={"section": 1 - section},
        device_id_type=MESH,
    )
    every_piece.wait_recv()
    out = pltpu.make_async_copy(land, arrived_out, loc_sem.at[1])
    out.start()
    for key in ((6, 1), (6, 2), (9, 0), (9, 3)):
        gk.arrived(*key)
    rh.finish()
    slot = dp.slot(1, 2)
    normalise(ks, slot, vblk, 2)

    def store(n):
        at = pl.ds(pl.multiple_of(n * rows, rows), rows)
        return pltpu.make_async_copy(xs.at[n], wg_out.at[at], wg_sem.at[n])

    def last(n, carry):
        at = pl.ds(pl.multiple_of(n * rows, rows), rows)
        term = lax.dot_general(vblk[:, at], cs[slot], (((0,), (0,)), ((), ())), preferred_element_type=F32)
        xs[n] = (wg[at, :] + term).astype(BF16)
        store(n).start()
        return carry

    lax.fori_loop(0, width // rows, last, 0)

    bg_out[...] = jnp.sum(bsum[...], 0, keepdims=True)
    column.arrived()
    ng_out[...] = column.total()

    every_piece.wait_send()
    for transfer in (gc, gk, rg, rh, stats, finished, column, terms):
        transfer.finish()
    keep.wait()
    for n in range(width // rows):
        store(n).wait()
    out.wait()


def finish_kernel(
    arrived, passed, grad, bias_grad, norm_grads, next_out, passed_out, wg_out, bg_out, ng_out
):
    wg_out[...] = grad[...].astype(F32)

    @pl.when(pl.program_id(0) == 0)
    def _():
        piece_rows = next_out.shape[0] // GROUP

        def body(a, carry):
            at = pl.ds(pl.multiple_of(a * piece_rows, piece_rows), piece_rows)
            for k in range(GROUP // 2):
                even, odd = arrived[a, 2 * k], arrived[a, 2 * k + 1]
                shared = swap_halves(even[piece_rows:].astype(F32), odd[piece_rows:].astype(F32))
                columns = (even[:piece_rows], jnp.concatenate(shared, axis=0).astype(BF16), odd[:piece_rows])
                for i, column in enumerate(columns):
                    next_out[at, (3 * k + i) * LANES : (3 * k + i + 1) * LANES] = column
            return carry

        lax.fori_loop(0, GROUP, body, 0)
        passed_out[...] = passed[...]
        bg_out[...] = bias_grad[...]
        ng_out[...] = norm_grads[...]


def shards(fwd_in, kept_in, cotangent, weight, bias, norm_gain, norm_shift):
    section_index = lax.axis_index("section")
    rows, cols = fwd_in.shape[3:]
    piece = (GROUP, GROUP, rows // GROUP * 3 // 2, LANES)
    any_spec = pl.BlockSpec(memory_space=pl.ANY)
    vmem_spec = pl.BlockSpec(memory_space=pltpu.VMEM)
    dma = pltpu.SemaphoreType.DMA
    shard = pltpu.VMEM((rows, cols), BF16)
    gathered = pltpu.VMEM((GROUP, rows, cols), BF16)
    two = pltpu.VMEM((2, rows, cols), BF16)
    arrived, passed, grad, bias_grad, norm_grads = pl.pallas_call(
        relay_kernel,
        name="relay",
        out_shape=(
            jax.ShapeDtypeStruct(piece, BF16),
            jax.ShapeDtypeStruct((rows, cols), BF16),
            jax.ShapeDtypeStruct((cols, cols), BF16),
            jax.ShapeDtypeStruct((1, cols), F32),
            jax.ShapeDtypeStruct((2, cols), F32),
        ),
        in_specs=[any_spec] * 4 + [vmem_spec] * 3,
        out_specs=(any_spec,) * 3 + (vmem_spec,) * 2,
        scratch_shapes=[
            gathered, gathered, gathered, pltpu.VMEM((cols, cols), BF16), shard, pltpu.VMEM((cols, cols), F32),
            pltpu.VMEM((7, rows, cols), BF16),
            two, two, two, shard, two, two, two, shard,
            shard, pltpu.VMEM((rows, cols), F32), pltpu.VMEM((rows, cols), F32), shard, pltpu.VMEM((rows, 128), F32),
            pltpu.VMEM((GROUP, 8, rows), F32), pltpu.VMEM((GROUP, 8, rows), F32), pltpu.VMEM((GROUP, 8, rows), F32),
            pltpu.VMEM((GROUP, 2, cols), F32), pltpu.VMEM((8, cols), F32),
            pltpu.VMEM(piece, BF16), pltpu.VMEM(piece, BF16),
            dma((5,)), dma((cols // rows,)),
            dma((7, 2)), dma((7, 2)), dma((7, 2)), dma((7, 2)), dma((10, 4)), dma((10, 4)),
            dma((16,)), dma((16,)), dma((16,)), dma((16,)),
            dma((7,)), dma((7,)), dma((7,)), dma((7,)), dma((7,)), dma((7,)), dma((7,)), dma((7,)),
            dma, dma,
        ],
        compiler_params=pltpu.CompilerParams(
            collective_id=0, has_side_effects=True, vmem_limit_bytes=60 * 2**20
        ),
    )(
        fwd_in.reshape(rows, cols),
        kept_in.reshape(rows, cols),
        cotangent.reshape(rows, cols),
        weight.reshape(cols, cols),
        bias.reshape(1, cols),
        norm_gain.reshape(1, cols),
        norm_shift.reshape(1, cols),
    )
    fixed = lambda *shape: pl.BlockSpec(shape, lambda i: (0,) * len(shape))
    tile = pl.BlockSpec((MXU, cols), lambda i: (i, 0))
    next_in, passed, weight_grad, bias_grad, norm_grads = pl.pallas_call(
        finish_kernel,
        name="finish",
        grid=(cols // MXU,),
        out_shape=(
            jax.ShapeDtypeStruct((rows, cols), BF16),
            jax.ShapeDtypeStruct((rows, cols), BF16),
            jax.ShapeDtypeStruct((cols, cols), F32),
            jax.ShapeDtypeStruct((1, cols), F32),
            jax.ShapeDtypeStruct((2, cols), F32),
        ),
        in_specs=[
            fixed(*piece),
            fixed(rows, cols),
            tile,
            fixed(1, cols),
            fixed(2, cols),
        ],
        out_specs=(fixed(rows, cols), fixed(rows, cols), tile, fixed(1, cols), fixed(2, cols)),
        compiler_params=pltpu.CompilerParams(vmem_limit_bytes=60 * 2**20),
    )(arrived, passed, grad, bias_grad, norm_grads)
    return (
        next_in.reshape(fwd_in.shape),
        passed.reshape(fwd_in.shape),
        weight_grad.reshape(1, cols, cols),
        bias_grad,
        norm_grads.reshape(1, 2, cols),
    )


def solution(mesh):
    placed = (
        P("section", "dp", "mp", None, None),
        P("section", "dp", "mp", None, None),
        P("section", "dp", "mp", None, None),
        P("section", "mp", "dp"),
        P("section", "dp"),
        P("section", "mp"),
        P("section", "mp"),
    )
    return jax.shard_map(
        shards,
        mesh=mesh,
        in_specs=placed,
        out_specs=(
            P("section", "dp", "mp", None, None),
            P("section", "dp", "mp", None, None),
            P("section", "mp", "dp"),
            P("section", "dp"),
            P("section", None, "mp"),
        ),
        check_vma=False,
    )
```

```python
import jax
import jax.numpy as jnp
from jax import lax
from jax.experimental import pallas as pl
from jax.experimental.pallas import tpu as pltpu
from jax.sharding import PartitionSpec as P

EPS = 1e-05
RING = 4
PAIR = 2
GROUP = RING * PAIR
TILE = 16
MXU = 256
LANES = 128
F32 = jnp.float32
BF16 = jnp.bfloat16
MESH = pl.DeviceIdType.MESH


class Spot:
    def __init__(self, group):
        self.group = group
        self.index = lax.axis_index(group)
        self.pair = lax.div(self.index, RING)
        self.ring = lax.rem(self.index, RING)

    def slot(self, pair_step, ring_step):
        pair = lax.rem(self.pair + pair_step, PAIR)
        return pair * RING + lax.rem(self.ring + ring_step + RING, RING)

    def device(self, pair_step, ring_step):
        return {self.group: self.slot(pair_step, ring_step)}


class Gather:
    def __init__(self, spot, buf, send_sem, recv_sem, far_by_pair, parts=2):
        self.spot, self.buf, self.far_by_pair, self.parts = spot, buf, far_by_pair, parts
        self.send_sem, self.recv_sem = send_sem, recv_sem
        self.part = buf.shape[1] // parts
        self.started = []

    def route(self, kind, c):
        step = 1 if c < self.parts // 2 else -1
        return {
            0: ((0, 0), (1, 0), (1, 0)),
            1: ((0, 0), (0, 1), (0, -1)),
            2: ((0, 0), (0, -1), (0, 1)),
            3: ((1, 0), (0, 1), (1, -1)),
            4: ((1, 0), (0, -1), (1, 1)),
            5: ((0, -step), (0, step), (0, 2)),
            7: ((0, -1), (1, 0), (1, -1)),
            9: ((1, -step), (0, step), (1, 2)),
            8: ((0, 1), (1, 0), (1, 1)),
            6: ((0, 2), (1, 0), (1, 2)) if self.far_by_pair else ((1, -step), (0, step), (1, 2)),
        }[kind]

    def copy(self, kind, c, landing):
        source, target, lands = self.route(kind, c)
        here = self.spot.slot(*(lands if landing else source))
        view = self.buf.at[here, pl.ds(c * self.part, self.part)]
        return pltpu.make_async_remote_copy(
            src_ref=view,
            dst_ref=view,
            send_sem=self.send_sem.at[kind, c],
            recv_sem=self.recv_sem.at[kind, c],
            device_id=self.spot.device(*target),
            device_id_type=MESH,
        )

    def start(self, kind, c):
        self.copy(kind, c, False).start()
        self.started.append((kind, c))

    def arrived(self, kind, c):
        self.copy(kind, c, True).wait_recv()

    def sent(self, kind):
        for c in (0, 1):
            self.copy(kind, c, False).wait_send()
            self.started.remove((kind, c))

    def finish(self):
        for kind, c in self.started:
            self.copy(kind, c, False).wait_send()
        self.started = []


class Scatter:
    def __init__(self, spot, stage, halves, left, right, crossed, send_sem, recv_sem):
        self.spot, self.stage = spot, stage
        self.halves, self.left, self.right, self.crossed = halves, left, right, crossed
        self.send_sem, self.recv_sem = send_sem, recv_sem
        self.half = halves.shape[1] // 2
        self.started = []

    def copy(self, kind, side, c):
        spot, rows = self.spot, pl.ds(c * self.half, self.half)
        step = 1 if c == 0 else -1
        source, target, lands = {
            0: (self.stage(side, 2), (0, step), self.halves.at[side]),
            1: (self.stage(side, 1), (0, 1), self.left.at[side]),
            2: (self.stage(side, -1), (0, -1), self.right.at[side]),
            3: (self.stage(side, 0), (1, 0), self.crossed),
        }[kind]
        sem = (kind * 2 + side) * 2 + c
        return pltpu.make_async_remote_copy(
            src_ref=source.at[rows],
            dst_ref=lands.at[rows],
            send_sem=self.send_sem.at[sem],
            recv_sem=self.recv_sem.at[sem],
            device_id=spot.device(*target),
            device_id_type=MESH,
        )

    def start(self, kind, side, c):
        self.copy(kind, side, c).start()
        self.started.append((kind, side, c))

    def arrived(self, kind, side, c):
        self.copy(kind, side, c).wait_recv()

    def finish(self):
        for key in self.started:
            self.copy(*key).wait_send()
        self.started = []


class Spread:
    def __init__(self, spot, buf, send_sem, recv_sem):
        self.spot, self.buf, self.send_sem, self.recv_sem = spot, buf, send_sem, recv_sem

    def copy(self, step, landing):
        me = self.spot.index
        other = lax.rem(me + step, GROUP)
        view = self.buf.at[lax.rem(me + GROUP - step, GROUP) if landing else me]
        return pltpu.make_async_remote_copy(
            src_ref=view,
            dst_ref=view,
            send_sem=self.send_sem.at[step - 1],
            recv_sem=self.recv_sem.at[step - 1],
            device_id={self.spot.group: other},
            device_id_type=MESH,
        )

    def start(self):
        for step in range(1, GROUP):
            self.copy(step, False).start()

    def arrived(self):
        for step in range(1, GROUP):
            self.copy(step, True).wait_recv()

    def finish(self):
        for step in range(1, GROUP):
            self.copy(step, False).wait_send()

    def total(self):
        result = self.buf[0]
        for i in range(1, GROUP):
            result = result + self.buf[i]
        return result


def swap_halves(first, second):
    left = lax.broadcasted_iota(jnp.int32, first.shape, 1) < LANES // 2
    return (
        jnp.where(left, first, pltpu.roll(second, LANES // 2, 1)),
        jnp.where(left, pltpu.roll(first, LANES // 2, 1), second),
    )


def tiles(count, body, size=TILE):
    def step(i, carry):
        body(pl.ds(pl.multiple_of(i * size, size), size))
        return carry

    lax.fori_loop(0, count // size, step, 0, unroll=4)


def relay_kernel(
    fwd, kept, cot, weight, bias, gain, shift,
    arrived_out, passed_out, wg_out, bg_out, ng_out,
    xs, ks, cs, w, kown, wg, gst, hhalf, hleft, hright, hcross, ghalf, gleft, gright, gcross,
    vblk, acc, accg, yout, cols, stat, fin, rowt, colg, bsum, pack, land,
    loc_sem, wg_sem,
    c_ss, c_rs, x_ss, x_rs, k_ss, k_rs, h_ss, h_rs, g_ss, g_rs,
    stat_ss, stat_rs, fin_ss, fin_rs, rowt_ss, rowt_rs, colg_ss, colg_rs, a_ss, a_rs,
):
    section = lax.axis_index("section")
    dp, mp = Spot("dp"), Spot("mp")
    rows, width = fwd.shape
    full = width * GROUP
    wide = width // 2

    loads = [
        pltpu.make_async_copy(cot, cs.at[mp.index], loc_sem.at[0]),
        pltpu.make_async_copy(fwd, xs.at[dp.index], loc_sem.at[1]),
        pltpu.make_async_copy(kept, ks.at[dp.index], loc_sem.at[2]),
        pltpu.make_async_copy(kept, kown, loc_sem.at[3]),
        pltpu.make_async_copy(weight, w, loc_sem.at[4]),
    ]
    for i in (1, 2, 0):
        loads[i].start()

    barrier = pltpu.get_barrier_semaphore()
    for spot in (mp, dp):
        for step in range(1, GROUP):
            pl.semaphore_signal(
                barrier, inc=1, device_id={spot.group: lax.rem(spot.index + step, GROUP)}, device_id_type=MESH
            )

    pl.semaphore_signal(barrier, inc=1, device_id={"section": 1 - section}, device_id_type=MESH)

    lane = lax.broadcasted_iota(jnp.int32, (TILE, 128), 1)

    def in_lanes(values):
        result = jnp.zeros((TILE, 128), F32)
        for i, value in enumerate(values):
            result = jnp.where(lane == i, value, result)
        return result

    def row_sums(at):
        x = xs[dp.index, at].astype(F32)
        k = ks[dp.index, at].astype(F32)
        sums = [jnp.sum(v, 1, keepdims=True) for v in (x, x * x, k, k * k)]
        cols[at] = in_lanes(sums)

    loads[1].wait()
    loads[2].wait()
    tiles(rows, row_sums)
    stat[mp.index] = jnp.transpose(cols[...])[0:8]
    loads[0].wait()
    pl.semaphore_wait(barrier, 2 * (GROUP - 1) + 1)

    gc = Gather(mp, cs, c_ss, c_rs, False)
    gx = Gather(dp, xs, x_ss, x_rs, True)
    gk = Gather(dp, ks, k_ss, k_rs, True, 4)
    stats = Spread(mp, stat, stat_ss, stat_rs)
    stats.start()
    for c in (0, 1):
        for gather in (gc, gx):
            gather.start(0, c)
            gather.start(1, c)
            gather.start(2, 1 - c)
    loads[4].start()
    loads[3].start()
    stats.arrived()
    sums = stats.total() / full
    mean_x, mean_k = sums[0:1], sums[2:3]
    inv_x = lax.rsqrt(sums[1:2] - mean_x * mean_x + EPS)
    inv_k = lax.rsqrt(sums[3:4] - mean_k * mean_k + EPS)
    row = lax.broadcasted_iota(jnp.int32, (8, rows), 0)
    fin[dp.index] = jnp.where(row == 0, mean_x, jnp.where(row == 1, inv_x, jnp.where(row == 2, mean_k, inv_k)))
    finished = Spread(dp, fin, fin_ss, fin_rs)
    finished.start()

    def forward(gather):
        gather.arrived(1, 0)
        gather.start(5, 0)
        gather.arrived(2, 1)
        gather.start(5, 1)

    for gather in (gc, gx):
        forward(gather)
    for c in (0, 1):
        for gather in (gc, gx):
            gather.arrived(0, c)
            gather.start(3, c)
            gather.start(4, c)
        if c == 0:
            for d in (0, 1):
                gx.arrived(5, d)
                gx.start(6, d)
    for c in range(3):
        gk.start(1, c)
        gk.start(2, 3 - c)
    for c in range(4):
        gk.start(0, c)
    gc.arrived(3, 0)
    gc.start(6, 0)
    gc.arrived(4, 1)
    gc.start(6, 1)

    def normalise(buf, slot, out, which):
        cols[:, 0:8] = jnp.transpose(fin[slot])

        def body(at):
            mean = cols[at, which : which + 1]
            inv = cols[at, which + 1 : which + 2]
            hat = (buf[slot, at].astype(F32) - mean) * inv
            out[at] = (hat * gain[...] + shift[...]).astype(BF16)

        tiles(rows, body)

    finished.arrived()
    for steps, kinds, sent in (
        ((0, 0), (), (0, 1, 2)),
        ((0, 1), ((2, 0),), (5,)),
        ((0, -1), ((1, 1),), ()),
        ((1, 0), (), (3, 4)),
        ((1, 1), ((4, 0), (4, 1)), ()),
        ((1, -1), ((3, 0), (3, 1)), ()),
        ((0, 2), (), (6,)),
        ((1, 2), ((6, 0), (6, 1)), ()),
    ):
        for key in kinds:
            gx.arrived(*key)
        for kind in sent:
            gx.sent(kind)
        slot = dp.slot(*steps)
        normalise(xs, slot, xs.at[slot], 0)
    loads[4].wait()
    for kind, c in ((1, 1), (2, 0), (3, 1), (4, 0), (5, 0), (5, 1), (6, 0), (6, 1)):
        gc.arrived(kind, c)
    loads[3].wait()

    def product_h(slot, acc):
        def body(n, carry):
            at = pl.ds(pl.multiple_of(n * wide, MXU), wide)
            acc[:, at] = jnp.dot(xs[slot], w[:, at], preferred_element_type=F32)
            return carry

        lax.fori_loop(0, width // wide, body, 0)

    def product_g(slot, acc):
        def body(n, carry):
            at = pl.ds(pl.multiple_of(n * wide, MXU), wide)
            acc[:, at] = lax.dot_general(
                cs[slot], w[at, :], (((1,), (1,)), ((), ())), preferred_element_type=F32
            )
            return carry

        lax.fori_loop(0, width // wide, body, 0)

    def product_w(pair_step, ring_step, fresh=False):
        slot = dp.slot(pair_step, ring_step)
        normalise(ks, slot, vblk, 2)

        def body(n, carry):
            at = pl.ds(pl.multiple_of(n * wide, MXU), wide)
            term = lax.dot_general(
                vblk[:, at], cs[slot], (((0,), (0,)), ((), ())), preferred_element_type=F32
            )
            wg[at, :] = term if fresh else wg[at, :] + term
            return carry

        lax.fori_loop(0, width // wide, body, 0)

    half = rows // 2

    def emit(stage, start, terms, acc):
        def body(i, carry):
            at = pl.ds(pl.multiple_of(start + i * TILE, TILE), TILE)
            value = acc[at]
            for term in terms:
                value = value + term[at].astype(F32)
            stage[at] = value.astype(BF16)
            return carry

        lax.fori_loop(0, half // TILE, body, 0, unroll=4)

    def stage_g(side, ring_step):
        place = {2: 0, 1: 1, -1: 2, 0: 3}[ring_step] * 2 + side
        return gst.at[place]

    def stage_h(side, ring_step):
        return xs.at[mp.slot(1 - side, ring_step)]

    rg = Scatter(dp, stage_g, ghalf, gleft, gright, gcross, g_ss, g_rs)
    rh = Scatter(mp, stage_h, hhalf, hleft, hright, hcross, h_ss, h_rs)
    work_g, work_h = (rg, product_g), (rh, product_h)

    def far(scatter, product, side):
        product(scatter.spot.slot(1 - side, 2), acc)
        for c in (0, 1):
            emit(scatter.stage(side, 2), c * half, [], acc)
            scatter.start(0, side, c)

    def near(scatter, product, side):
        product(scatter.spot.slot(1 - side, 1), acc)
        scatter.arrived(0, side, 0)
        for c in (0, 1):
            emit(scatter.stage(side, 1), c * half, [] if c else [scatter.halves.at[side]], acc)
            scatter.start(1, side, c)
        product(scatter.spot.slot(1 - side, -1), acc)
        for c in (0, 1):
            if c:
                scatter.arrived(0, side, 1)
            emit(scatter.stage(side, -1), c * half, [scatter.halves.at[side]] if c else [], acc)
            scatter.start(2, side, c)

    def cross(scatter, c, acc):
        scatter.arrived(1, 0, c)
        scatter.arrived(2, 0, c)
        emit(scatter.stage(0, 0), c * half, [scatter.left.at[0], scatter.right.at[0]], acc)
        scatter.start(3, 0, c)

    far(*work_g, 0)
    far(*work_h, 0)
    for kind, c in ((1, 0), (2, 3)):
        gk.arrived(kind, c)
        gk.start(kind + 6, c)
    near(*work_g, 0)
    near(*work_h, 0)
    far(*work_g, 1)
    far(*work_h, 1)
    gk.start(1, 3)
    gk.start(2, 0)
    gk.start(5, 0)
    gk.start(5, 3)
    gk.arrived(1, 1)
    gk.start(5, 1)
    gk.arrived(2, 2)
    gk.start(5, 2)
    product_g(dp.slot(1, 0), accg)
    cross(rg, 0, accg)
    near(*work_g, 1)
    near(*work_h, 1)
    cross(rg, 1, accg)
    product_h(mp.slot(1, 0), accg)
    cross(rh, 0, accg)
    cross(rh, 1, accg)
    for c in range(4):
        gk.arrived(0, c)
        if c != 0:
            gk.start(3, c)
        if c != 3:
            gk.start(4, c)
    for c in range(4):
        gk.arrived(5, c)
        if c in (1, 2):
            gk.start(6, c)
    for kind, c in ((7, 0), (8, 3)):
        gk.arrived(kind, c)
        gk.start(9, c)

    bsum[...] = jnp.zeros_like(bsum)

    def add_block(slot, carry):
        def add(at):
            c = cs[slot, at].astype(F32)
            bsum[...] += c[0:8] + c[8:16]

        tiles(rows, add)
        return carry

    lax.fori_loop(0, GROUP, add_block, 0)
    product_w(0, 0, True)
    product_w(1, 0)
    product_w(0, 2)
    for kind, c in ((2, 1), (2, 0), (1, 2), (1, 3)):
        gk.arrived(kind, c)
    product_w(0, 1)
    product_w(0, -1)

    def whole(scatter, acc, finish):
        for c in (0, 1):
            for kind, side in ((1, 1), (2, 1), (3, 0)):
                scatter.arrived(kind, side, c)

        def body(at):
            value = acc[at]
            for term in (scatter.left.at[1], scatter.right.at[1], scatter.crossed):
                value = value + term[at].astype(F32)
            finish(at, value)

        tiles(rows, body)

    def hat_kept(at):
        return (kown[at].astype(F32) - cols[at, 2:3]) * cols[at, 3:4]

    def finish_g(at, value):
        hat = hat_kept(at)
        colg[dp.index, 0:1] += jnp.sum(value * hat, 0, keepdims=True)
        colg[dp.index, 1:2] += jnp.sum(value, 0, keepdims=True)
        accg[at] = value
        scaled = value * gain[...]
        terms = [jnp.sum(v, 1, keepdims=True) for v in (scaled, scaled * hat)]
        lanes = in_lanes(terms)
        cols[at, 8:16] = lanes[:, 0:8]

    product_g(dp.slot(0, 0), accg)
    product_h(mp.slot(0, 0), acc)
    cols[:, 0:8] = jnp.transpose(fin[dp.index])
    colg[dp.index] = jnp.zeros(colg.shape[1:], F32)
    whole(rg, accg, finish_g)
    terms = Spread(mp, rowt, rowt_ss, rowt_rs)
    rowt[mp.index] = jnp.transpose(cols[...])[8:16]
    terms.start()
    column = Spread(dp, colg, colg_ss, colg_rs)
    column.start()

    piece_rows = rows // GROUP
    first = section == 0
    row_at = jnp.where(first, mp.index, dp.index)
    col_at = jnp.where(first, dp.index, mp.index)

    def piece(i):
        j = lax.rem(i + dp.index * GROUP + mp.index, GROUP * GROUP)
        b, f = lax.div(j, GROUP), lax.rem(j, GROUP)
        return pltpu.make_async_remote_copy(
            src_ref=pack.at[b, f],
            dst_ref=land.at[row_at, col_at],
            send_sem=a_ss,
            recv_sem=a_rs,
            device_id={"section": 1 - section, "dp": jnp.where(first, b, f), "mp": jnp.where(first, f, b)},
            device_id_type=MESH,
        )

    def send_piece(i, carry):
        piece(i).start()
        return carry

    odd = lax.rem(col_at, 2) == 1
    low = lax.broadcasted_iota(jnp.int32, (piece_rows, LANES), 1) < LANES // 2

    def halves(value):
        return value[: piece_rows // 2], value[piece_rows // 2 :]

    def relay(values):
        def packing(b, carry):
            at = pl.ds(pl.multiple_of(b * piece_rows, piece_rows), piece_rows)
            sent = values[at]
            for k in range(GROUP // 2):
                left, shared, right = (sent[:, (3 * k + i) * LANES : (3 * k + i + 1) * LANES] for i in range(3))
                turned = [pltpu.roll(v, LANES // 2, 1) for v in (left, shared, right)]
                early = jnp.where(odd, jnp.where(low, turned[0], turned[1]), left)
                later = jnp.where(odd, right, jnp.where(low, turned[1], turned[2]))
                early_half = swap_halves(*halves(jnp.where(odd, left, shared)))[0]
                later_half = swap_halves(*halves(jnp.where(odd, shared, right)))[1]
                pack[b, 2 * k, 0:piece_rows] = early.astype(BF16)
                pack[b, 2 * k + 1, 0:piece_rows] = later.astype(BF16)
                pack[b, 2 * k, piece_rows:] = early_half.astype(BF16)
                pack[b, 2 * k + 1, piece_rows:] = later_half.astype(BF16)
            return carry

        lax.fori_loop(0, GROUP, packing, 0)
        lax.fori_loop(0, GROUP * GROUP, send_piece, 0)

    def finish_h(at, value):
        acc[at] = value + bias[...]

    whole(rh, acc, finish_h)

    @pl.when(first)
    def _():
        relay(acc)

    terms.arrived()
    cols[:, 8:16] = jnp.transpose(terms.total() / full)

    def input_grad(at):
        hat = hat_kept(at)
        scaled = accg[at] * gain[...]
        accg[at] = cols[at, 3:4] * (scaled - cols[at, 8:9] - hat * cols[at, 9:10])

    tiles(rows, input_grad)

    @pl.when(section == 1)
    def _():
        relay(accg)

    def keeping(at):
        yout[at] = jnp.where(first, accg[at], acc[at]).astype(BF16)

    tiles(rows, keeping)
    keep = pltpu.make_async_copy(yout, passed_out, loc_sem.at[0])
    keep.start()

    for steps, kinds in (
        ((1, 1), ((4, 0), (4, 1), (4, 2))),
        ((1, -1), ((3, 1), (3, 2), (3, 3))),
    ):
        for key in kinds:
            gk.arrived(*key)
        product_w(*steps)
    every_piece = pltpu.make_async_remote_copy(
        src_ref=pack,
        dst_ref=land,
        send_sem=a_ss,
        recv_sem=a_rs,
        device_id={"section": 1 - section},
        device_id_type=MESH,
    )
    for key in ((6, 1), (6, 2), (9, 0), (9, 3)):
        gk.arrived(*key)
    rh.finish()
    slot = dp.slot(1, 2)
    normalise(ks, slot, vblk, 2)

    def store(n):
        at = pl.ds(pl.multiple_of(n * rows, rows), rows)
        return pltpu.make_async_copy(xs.at[n], wg_out.at[at], wg_sem.at[n])

    def last(n, carry):
        at = pl.ds(pl.multiple_of(n * rows, rows), rows)
        term = lax.dot_general(vblk[:, at], cs[slot], (((0,), (0,)), ((), ())), preferred_element_type=F32)
        xs[n] = (wg[at, :] + term).astype(BF16)
        store(n).start()
        return carry

    lax.fori_loop(0, width // rows, last, 0)
    every_piece.wait_recv()
    out = pltpu.make_async_copy(land, arrived_out, loc_sem.at[1])
    out.start()

    bg_out[...] = jnp.sum(bsum[...], 0, keepdims=True)
    column.arrived()
    ng_out[...] = column.total()

    every_piece.wait_send()
    for transfer in (gc, gk, rg, rh, stats, finished, column, terms):
        transfer.finish()
    keep.wait()
    for n in range(width // rows):
        store(n).wait()
    out.wait()


def finish_kernel(
    arrived, passed, grad, bias_grad, norm_grads, next_out, passed_out, wg_out, bg_out, ng_out
):
    wg_out[...] = grad[...].astype(F32)

    @pl.when(pl.program_id(0) == 0)
    def _():
        piece_rows = next_out.shape[0] // GROUP

        def body(a, carry):
            at = pl.ds(pl.multiple_of(a * piece_rows, piece_rows), piece_rows)
            for k in range(GROUP // 2):
                even, odd = arrived[a, 2 * k], arrived[a, 2 * k + 1]
                shared = swap_halves(even[piece_rows:].astype(F32), odd[piece_rows:].astype(F32))
                columns = (even[:piece_rows], jnp.concatenate(shared, axis=0).astype(BF16), odd[:piece_rows])
                for i, column in enumerate(columns):
                    next_out[at, (3 * k + i) * LANES : (3 * k + i + 1) * LANES] = column
            return carry

        lax.fori_loop(0, GROUP, body, 0)
        passed_out[...] = passed[...]
        bg_out[...] = bias_grad[...]
        ng_out[...] = norm_grads[...]


def shards(fwd_in, kept_in, cotangent, weight, bias, norm_gain, norm_shift):
    section_index = lax.axis_index("section")
    rows, cols = fwd_in.shape[3:]
    piece = (GROUP, GROUP, rows // GROUP * 3 // 2, LANES)
    any_spec = pl.BlockSpec(memory_space=pl.ANY)
    vmem_spec = pl.BlockSpec(memory_space=pltpu.VMEM)
    dma = pltpu.SemaphoreType.DMA
    shard = pltpu.VMEM((rows, cols), BF16)
    gathered = pltpu.VMEM((GROUP, rows, cols), BF16)
    two = pltpu.VMEM((2, rows, cols), BF16)
    arrived, passed, grad, bias_grad, norm_grads = pl.pallas_call(
        relay_kernel,
        name="relay",
        out_shape=(
            jax.ShapeDtypeStruct(piece, BF16),
            jax.ShapeDtypeStruct((rows, cols), BF16),
            jax.ShapeDtypeStruct((cols, cols), BF16),
            jax.ShapeDtypeStruct((1, cols), F32),
            jax.ShapeDtypeStruct((2, cols), F32),
        ),
        in_specs=[any_spec] * 4 + [vmem_spec] * 3,
        out_specs=(any_spec,) * 3 + (vmem_spec,) * 2,
        scratch_shapes=[
            gathered, gathered, gathered, pltpu.VMEM((cols, cols), BF16), shard, pltpu.VMEM((cols, cols), F32),
            pltpu.VMEM((7, rows, cols), BF16),
            two, two, two, shard, two, two, two, shard,
            shard, pltpu.VMEM((rows, cols), F32), pltpu.VMEM((rows, cols), F32), shard, pltpu.VMEM((rows, 128), F32),
            pltpu.VMEM((GROUP, 8, rows), F32), pltpu.VMEM((GROUP, 8, rows), F32), pltpu.VMEM((GROUP, 8, rows), F32),
            pltpu.VMEM((GROUP, 2, cols), F32), pltpu.VMEM((8, cols), F32),
            pltpu.VMEM(piece, BF16), pltpu.VMEM(piece, BF16),
            dma((5,)), dma((cols // rows,)),
            dma((7, 2)), dma((7, 2)), dma((7, 2)), dma((7, 2)), dma((10, 4)), dma((10, 4)),
            dma((16,)), dma((16,)), dma((16,)), dma((16,)),
            dma((7,)), dma((7,)), dma((7,)), dma((7,)), dma((7,)), dma((7,)), dma((7,)), dma((7,)),
            dma, dma,
        ],
        compiler_params=pltpu.CompilerParams(
            collective_id=0, has_side_effects=True, vmem_limit_bytes=60 * 2**20
        ),
    )(
        fwd_in.reshape(rows, cols),
        kept_in.reshape(rows, cols),
        cotangent.reshape(rows, cols),
        weight.reshape(cols, cols),
        bias.reshape(1, cols),
        norm_gain.reshape(1, cols),
        norm_shift.reshape(1, cols),
    )
    fixed = lambda *shape: pl.BlockSpec(shape, lambda i: (0,) * len(shape))
    tile = pl.BlockSpec((MXU, cols), lambda i: (i, 0))
    next_in, passed, weight_grad, bias_grad, norm_grads = pl.pallas_call(
        finish_kernel,
        name="finish",
        grid=(cols // MXU,),
        out_shape=(
            jax.ShapeDtypeStruct((rows, cols), BF16),
            jax.ShapeDtypeStruct((rows, cols), BF16),
            jax.ShapeDtypeStruct((cols, cols), F32),
            jax.ShapeDtypeStruct((1, cols), F32),
            jax.ShapeDtypeStruct((2, cols), F32),
        ),
        in_specs=[
            fixed(*piece),
            fixed(rows, cols),
            tile,
            fixed(1, cols),
            fixed(2, cols),
        ],
        out_specs=(fixed(rows, cols), fixed(rows, cols), tile, fixed(1, cols), fixed(2, cols)),
        compiler_params=pltpu.CompilerParams(vmem_limit_bytes=60 * 2**20),
    )(arrived, passed, grad, bias_grad, norm_grads)
    return (
        next_in.reshape(fwd_in.shape),
        passed.reshape(fwd_in.shape),
        weight_grad.reshape(1, cols, cols),
        bias_grad,
        norm_grads.reshape(1, 2, cols),
    )


def solution(mesh):
    placed = (
        P("section", "dp", "mp", None, None),
        P("section", "dp", "mp", None, None),
        P("section", "dp", "mp", None, None),
        P("section", "mp", "dp"),
        P("section", "dp"),
        P("section", "mp"),
        P("section", "mp"),
    )
    return jax.shard_map(
        shards,
        mesh=mesh,
        in_specs=placed,
        out_specs=(
            P("section", "dp", "mp", None, None),
            P("section", "dp", "mp", None, None),
            P("section", "mp", "dp"),
            P("section", "dp"),
            P("section", None, "mp"),
        ),
        check_vma=False,
    )
```
